256 devices in a mesh: ctx: 32 (over y, z), kvh: 8 (over x, core).
Axes of the slice: x: 4, y: 4, z: 8, core: 2. Of those that a mesh axis runs over, the one named last changes fastest.
Arguments:
- queries: bfloat16 [64, 64, 8, 1024], P('ctx', None, 'kvh'), may hold values from -92 to 92
- resp_keys: bfloat16 [64, 64, 8, 128], P('ctx', None, 'kvh'), may hold values from -6 to 6
- resp_values: bfloat16 [64, 64, 8, 128], P('ctx', None, 'kvh'), may hold values from -6 to 6
- prefix_keys: bfloat16 [32768, 8, 128], P('ctx', 'kvh'), may hold values from -6 to 6
- prefix_values: bfloat16 [32768, 8, 128], P('ctx', 'kvh'), may hold values from -6 to 6
- prefix_len: int32 [4], replicated, may hold values from 2048 to 8192, as said below
- prompt_of: int32 [64], replicated, may hold values from 0 to 3, as said below
- out_weight: bfloat16 [8192, 8192], P('kvh', 'ctx'), may hold values from -0.0625 to 0.0625
Outputs:
- attended: bfloat16 [64, 64, 8, 1024], P('ctx', None, 'kvh')
- projected: bfloat16 [4096, 8192], P('ctx', 'kvh')
The draws below stay inside these ranges and needn't reach their ends.
Inputs may be any that keep to these rules, and one draw needn't show every extreme that they name: `prefix_len`: every prompt's length lies in the range and one prompt has exactly 8192. `prompt_of`: every prompt is named by 16 responses; the 2 responses of one index of ctx name each prompt at most 1 times, and some prompt exactly 1 times on every index.
All inputs are finite; a program needn't handle non-finite values.
Results may differ from the reference program's by a relative error of at most 0.038.
Values may be sent and summed in bfloat16 or wider, within the bound.
A program may use at most 128 MiB of HBM per device.

```python
import math
import jax
import jax.numpy as jnp
from jax import lax

D = 8192
HQ = 8
HD = 128
P_SIZE = 4
RLEN = 64
LMAX = 8192
KVH = 8
R = 64
RESP_DEV = 2
SLOTS_DEV = 1024


def draw_resp_keys(key, part):
    key = jax.random.fold_in(key, 3)
    drawn = jax.random.normal(key, (R, RLEN, KVH, HD), jnp.float32) * 1.5
    return jnp.clip(drawn, -6.0, 6.0).astype(jnp.bfloat16)


def draw_queries(key, part):
    key = jax.random.fold_in(key, 4)
    drawn = jax.random.normal(key, (R, RLEN, KVH, HQ * HD), jnp.float32)
    return jnp.clip(drawn, -5.0, 5.0).astype(jnp.bfloat16)


def draw_prefix_len(key, part):
    key = jax.random.fold_in(key, 7)
    first_key, second_key = jax.random.split(key)
    lengths = jax.random.randint(first_key, (P_SIZE,), LMAX // 4, LMAX + 1)
    longest = jax.random.randint(second_key, (), 0, P_SIZE)
    return jnp.where(jnp.arange(P_SIZE) == longest, LMAX, lengths).astype(jnp.int32)


def draw_prompt_of(key, part):
    key = jax.random.fold_in(key, 5)
    first_key, second_key = jax.random.split(key)
    relabel = jax.random.permutation(first_key, P_SIZE)
    device_count = R // RESP_DEV

    def one_row(row_key):
        return jax.random.permutation(row_key, RESP_DEV)
    within = jax.vmap(one_row)(jax.random.split(second_key, device_count))
    devices = jnp.arange(device_count)[:, None]
    slot_prompt = (devices * RESP_DEV + within) % P_SIZE
    return relabel[slot_prompt].reshape(R).astype(jnp.int32)


def steps_of(own_key, dims, cuts, least, largest):
    level = 1.0
    for axis_at, blocks in cuts:
        draws = jax.random.uniform(jax.random.fold_in(jax.random.fold_in(own_key, 6), axis_at), (blocks,), jnp.float32, least / len(cuts), largest / len(cuts))
        level = level * jnp.repeat(jnp.exp(draws), dims[axis_at] // blocks).reshape((-1,) + (1,) * (len(dims) - 1 - axis_at))
    return level


def noise(key, shape, width, limit, pieces=(), held_as=jnp.bfloat16):
    values = width * jax.random.normal(key, shape, jnp.float32)
    if pieces:
        values = values * steps_of(key, shape, pieces, -0.22, 0.18)
    return jnp.clip(values, -limit, limit).astype(held_as)


def setup_inputs(seed: int = 0) -> dict:
    splits = jax.random.split(jax.random.key(seed), 9)
    return {
        "queries": draw_queries(jax.random.fold_in(splits[8], 71), 0),
        "resp_keys": draw_resp_keys(jax.random.fold_in(splits[8], 71), 0),
        "resp_values": noise(splits[2], (R, RLEN, KVH, HD), 1.0, 6.0, ((0, 32), (2, 8))),
        "prefix_keys": noise(splits[3], (P_SIZE * LMAX, KVH, HD), 1.0, 6.0, ((0, 32), (1, 8))),
        "prefix_values": noise(splits[4], (P_SIZE * LMAX, KVH, HD), 1.0, 6.0, ((0, 32), (1, 8))),
        "prefix_len": draw_prefix_len(jax.random.fold_in(splits[8], 71), 0),
        "prompt_of": draw_prompt_of(jax.random.fold_in(splits[8], 71), 0),
        "out_weight": noise(splits[7], (KVH * HQ * HD, D), (KVH * HQ * HD) ** -0.5, 0.0625, ((0, 8), (1, 32))),
    }


MASKED = -1e+30

def partial_block(query_rows, keys, values, live):
    scores = jnp.einsum('thd,sd->ths', query_rows.astype(jnp.float32), keys.astype(jnp.float32)) * (1.0 / math.sqrt(HD))
    scores = jnp.where(live, scores, MASKED)
    peak = lax.optimization_barrier(jnp.max(scores, axis=-1))
    weights = jnp.where(live, jnp.exp(scores - peak[..., None]), 0.0)
    totals = lax.optimization_barrier(jnp.sum(weights, axis=-1))
    rounded = lax.optimization_barrier(weights.astype(jnp.bfloat16)).astype(jnp.float32)
    mixed = jnp.einsum('ths,sd->thd', rounded, values.astype(jnp.float32))
    return (mixed, peak, totals)

def one_response(response, queries, resp_keys, resp_values, prefix_keys, prefix_values, prefix_len, prompt_of):
    prompt = prompt_of[response]
    start = (prompt * LMAX).astype(jnp.int32)
    near_keys = lax.dynamic_slice_in_dim(prefix_keys, start, LMAX, 0)
    near_values = lax.dynamic_slice_in_dim(prefix_values, start, LMAX, 0)
    holders = LMAX // SLOTS_DEV
    positions = jnp.arange(LMAX, dtype=jnp.int32).reshape(holders, SLOTS_DEV)
    live_slots = positions < prefix_len[prompt]
    causal = jnp.arange(RLEN)[:, None] >= jnp.arange(RLEN)[None, :]

    def per_head(query_group, own_keys, own_values, group_keys, group_values):
        query_rows = query_group.reshape(RLEN, HQ, HD)
        own_mixed, own_peak, own_totals = partial_block(query_rows, own_keys, own_values, causal[:, None, :])

        def per_block(block_keys, block_values, block_live):
            mixed, peak, totals = partial_block(query_rows, block_keys, block_values, block_live[None, None, :])
            mixed = lax.optimization_barrier(mixed.astype(jnp.bfloat16)).astype(jnp.float32)
            return (mixed, peak, totals)
        far_mixed, far_peak, far_totals = jax.vmap(per_block)(group_keys.reshape(holders, SLOTS_DEV, HD), group_values.reshape(holders, SLOTS_DEV, HD), live_slots)
        highest = jnp.maximum(own_peak, lax.optimization_barrier(jnp.max(far_peak, axis=0)))
        own_scale = jnp.exp(own_peak - highest)
        far_scale = jnp.exp(far_peak - highest[None])
        numerator = own_scale[..., None] * own_mixed + lax.optimization_barrier(jnp.sum(far_scale[..., None] * far_mixed, axis=0))
        denominator = own_scale * own_totals + lax.optimization_barrier(jnp.sum(far_scale * far_totals, axis=0))
        return (numerator / denominator[..., None]).astype(jnp.bfloat16).reshape(RLEN, HQ * HD)
    return jax.vmap(per_head, in_axes=(1, 1, 1, 1, 1), out_axes=1)(queries[response], resp_keys[response], resp_values[response], near_keys, near_values)

def reference(queries, resp_keys, resp_values, prefix_keys, prefix_values, prefix_len, prompt_of, out_weight):

    def step_fn(response):
        return one_response(response, queries, resp_keys, resp_values, prefix_keys, prefix_values, prefix_len, prompt_of)
    attended = lax.map(step_fn, jnp.arange(R, dtype=jnp.int32))
    flat_rows = attended.reshape(R * RLEN, KVH * HQ * HD)
    projected = jnp.dot(flat_rows, out_weight, preferred_element_type=jnp.float32).astype(jnp.bfloat16)
    return (attended, projected)
```

```python
import math

import jax
import jax.numpy as jnp
from jax import lax
from jax.experimental import pallas as pl
from jax.experimental.pallas import tpu as pltpu
from jax.sharding import PartitionSpec as P

MESH = pl.DeviceIdType.MESH
NY, NZ, NX = 4, 8, 4
TOK, HD, SLOTS = 64, 128, 1024
OWN = 2 * TOK
LINE = NZ * OWN
RANKS = 16
COLS = 256
MASKED = -1e30
SCALE2 = math.log2(math.e) / math.sqrt(HD)
TILE = 256
NT = (((1,), (1,)), ((), ()))
F32, BF16 = jnp.float32, jnp.bfloat16


def dot(a, b):
    return jnp.dot(a, b, preferred_element_type=F32)


def kernel(
    len_ref, prompt_ref, q_ref, rk_ref, rv_ref, k_ref, v_ref, w_ref,
    att_ref, proj_ref,
    src_tab, rank_tab,
    kv, qline, qsend, qarr, qh, acc, peak, own_o, own_lse, obuf, lbuf, osend, lsend, oarr, larr,
    abuf, wbuf, cacc, csend, crecv, xsend, xrecv, zsend, zrecv,
    local_sem, q1_s, q1_r, q2_s, q2_r, kv_s, kv_r, w_s, w_r, o_s, o_r, l_s, l_r, a_s, a_r, c_s, c_r, x_s, x_r, z_s, z_r,
):
    ctx, kvh = lax.axis_index("ctx"), lax.axis_index("kvh")
    y, z = lax.div(ctx, NZ), lax.rem(ctx, NZ)
    x, core = lax.div(kvh, 2), lax.rem(kvh, 2)
    sibling = x * 2 + 1 - core

    def z_at(d):
        return lax.rem(z + d + NZ, NZ)

    def y_at(d):
        return lax.rem(y + d, NY)

    def on_line(zz, head=None):
        return (y * NZ + zz, kvh if head is None else head)

    def on_column(yy):
        return (yy * NZ + z, kvh)

    def remote(src, dst, ss, rs, dev):
        return pltpu.make_async_remote_copy(
            src_ref=src, dst_ref=dst, send_sem=ss, recv_sem=rs, device_id=dev, device_id_type=MESH
        )

    locals_ = [
        pltpu.make_async_copy(src, dst, local_sem.at[i])
        for i, (src, dst) in enumerate([
            (k_ref, kv.at[0, 0, pl.ds(0, SLOTS)]),
            (rk_ref, kv.at[0, 0, pl.ds(SLOTS, OWN)]),
            (v_ref, kv.at[0, 1, pl.ds(0, SLOTS)]),
            (rv_ref, kv.at[0, 1, pl.ds(SLOTS, OWN)]),
            (q_ref.at[:, pl.ds(pl.multiple_of(z * HD, HD), HD)], qline.at[z]),
            (w_ref, wbuf.at[y]),
        ])
    ]
    for copy in locals_:
        copy.start()

    barrier = pltpu.get_barrier_semaphore()
    greeted = (
        [on_line(z_at(d)) for d in range(1, NZ)]
        + [on_line(z_at(d), sibling) for d in range(NZ)]
        + [on_column(y_at(d)) for d in range(1, NY)]
        + [(ctx, lax.rem(x + d, NX) * 2 + core) for d in range(1, NX)]
    )
    for dev in greeted:
        pl.semaphore_signal(barrier, inc=1, device_id=dev, device_id_type=MESH)
    pl.semaphore_wait(barrier, len(greeted))

    q1 = []
    for d in range(1, NZ):
        to = z_at(d)
        q1.append(remote(
            q_ref.at[:, pl.ds(pl.multiple_of(to * HD, HD), HD)], qline.at[z],
            q1_s.at[d - 1], q1_r.at[d - 1], on_line(to),
        ))
    for copy in q1:
        copy.start()

    right, left = on_line(z_at(1)), on_line(z_at(-1))

    def hop(src, dst, part, way):
        n = {1: 0, 2: 2, 3: 4, 4: 0, 5: 2, 6: 4, 7: 6}[dst] + (part if dst < 7 else 0)
        return remote(kv.at[src, part], kv.at[dst, part], kv_s.at[way, n], kv_r.at[way, n], left if way else right)

    hops = {}
    for part in range(2):
        for dst in range(1, 4):
            hops[dst, part] = hop(dst - 1, dst, part, 0)
        for dst in range(4, 7):
            hops[dst, part] = hop(0 if dst == 4 else dst - 1, dst, part, 1)
    hops[7, 0] = hop(3, 7, 0, 0)
    hops[7, 1] = hop(6, 7, 1, 1)

    for part in range(2):
        locals_[2 * part].wait()
        locals_[2 * part + 1].wait()
        hops[1, part].start()
        hops[4, part].start()

    run = jnp.int32(0)
    through = []
    for s in range(NY * NZ):
        named = (prompt_ref[2 * s] == y) | (prompt_ref[2 * s + 1] == y)
        rank_tab[s] = jnp.minimum(run, RANKS - 1)
        run = run + named.astype(jnp.int32)
        through.append(run)
    for j in range(RANKS):
        src = jnp.int32(0)
        for s in range(NY * NZ):
            src = src + (through[s] <= j).astype(jnp.int32)
        src_tab[j] = jnp.minimum(src, NY * NZ - 1)

    locals_[4].wait()
    for copy in q1:
        copy.wait_recv()

    def pick(zz, prompt):
        first = prompt_ref[(y * NZ + zz) * 2] == prompt
        return jnp.where(first, qline[zz, 0:TOK], qline[zz, TOK:OWN])

    q2 = []
    for d in range(1, NY):
        def fill(zz, carry, d=d):
            qsend[d - 1, zz] = pick(zz, y_at(d))
            return carry
        lax.fori_loop(0, NZ, fill, 0)
        copy = remote(
            qsend.at[d - 1], qarr.at[pl.ds(y * NZ, NZ)], q2_s.at[d - 1], q2_r.at[d - 1], on_column(y_at(d))
        )
        copy.start()
        q2.append(copy)

    def keep(zz, carry):
        qarr[y * NZ + zz] = pick(zz, y)
        return carry
    lax.fori_loop(0, NZ, keep, 0)

    locals_[5].wait()
    wy = [
        remote(wbuf.at[y], wbuf.at[y], w_s.at[d - 1], w_r.at[d - 1], on_column(y_at(d))) for d in range(1, NY)
    ]
    for copy in wy:
        copy.start()

    def own_block(slot, zz):
        scores = lax.dot_general(qline[zz], kv[slot, 0, SLOTS:SLOTS + OWN], NT, preferred_element_type=F32) * SCALE2
        row = lax.broadcasted_iota(jnp.int32, (OWN, OWN), 0)
        col = lax.broadcasted_iota(jnp.int32, (OWN, OWN), 1)
        live = (row >= col) & ((row < TOK) | (col >= TOK))
        scores = jnp.where(live, scores, MASKED)
        top = jnp.max(scores, axis=1, keepdims=True)
        weights = jnp.where(live, jnp.exp2(scores - top), 0.0)
        total = jnp.sum(weights, axis=1, keepdims=True)
        own_o[zz] = dot(weights.astype(BF16), kv[slot, 1, SLOTS:SLOTS + OWN]) / total
        own_lse[zz] = jnp.broadcast_to(top + jnp.log2(total), (OWN, HD))

    live_len = len_ref[y]
    ones = jnp.ones((SLOTS, HD), BF16)

    def attend(slot, block, first=False):
        live = block * SLOTS + lax.broadcasted_iota(jnp.int32, (1, SLOTS), 1) < live_len

        def tile(i, carry):
            rows = pl.ds(pl.multiple_of(i * TILE, TILE), TILE)
            scores = lax.dot_general(qh[rows], kv[slot, 0, 0:SLOTS], NT, preferred_element_type=F32)
            scores = jnp.where(live, scores * SCALE2, MASKED)
            top = jnp.max(scores, axis=1, keepdims=True)
            if not first:
                before = peak[rows]
                top = jnp.maximum(before[:, 0:1], top)
            weights = jnp.exp2(scores - top).astype(BF16)
            mixed = dot(weights, jnp.concatenate([kv[slot, 1, 0:SLOTS], ones], axis=1))
            top = jnp.broadcast_to(top, (TILE, HD))
            if not first:
                fade = jnp.exp2(before - top)
                mixed = mixed + acc[rows] * jnp.concatenate([fade, fade], axis=1)
            acc[rows] = mixed
            peak[rows] = top
            return carry
        lax.fori_loop(0, LINE // TILE, tile, 0)

    own_block(0, z)
    for copy in q2:
        copy.wait_recv()
    for j in range(RANKS):
        qh[j * TOK:(j + 1) * TOK] = qarr[src_tab[j]]
    attend(0, z, first=True)

    for step in range(1, 4):
        for part in range(2):
            for dst, after in ((step, step + 1 if step < 3 else 7), (step + 3, step + 4)):
                hops[dst, part].wait_recv()
                if step < 3 or part == (dst == 6):
                    hops[after, part].start()
        for slot, zz in ((step, z_at(-step)), (step + 3, z_at(step))):
            own_block(slot, zz)
            attend(slot, zz)
    for part in range(2):
        hops[7, part].wait_recv()
    own_block(7, z_at(4))
    attend(7, z_at(4))

    eye = lax.broadcasted_iota(jnp.int32, (TOK, HD), 0) == lax.broadcasted_iota(jnp.int32, (TOK, HD), 1)

    def finish(j, carry):
        rows = pl.ds(pl.multiple_of(j * TOK, TOK), TOK)
        total = acc[rows, HD:2 * HD]
        obuf[j] = (acc[rows, 0:HD] / total).astype(BF16)
        lse = jnp.sum(jnp.where(eye, peak[rows] + jnp.log2(total), 0.0), axis=0, keepdims=True)
        lbuf[j] = jnp.broadcast_to(lse, (8, HD))
        return carry
    lax.fori_loop(0, RANKS, finish, 0)

    back = []
    for d in range(1, NY):
        def put(zz, carry, d=d):
            rank = rank_tab[y_at(d) * NZ + zz]
            osend[d - 1, zz] = obuf[rank]
            lsend[d - 1, zz] = lbuf[rank]
            return carry
        lax.fori_loop(0, NZ, put, 0)
        back.append(remote(osend.at[d - 1], oarr.at[y], o_s.at[d - 1], o_r.at[d - 1], on_column(y_at(d))))
        back.append(remote(lsend.at[d - 1], larr.at[y], l_s.at[d - 1], l_r.at[d - 1], on_column(y_at(d))))
        back[-2].start()
        back[-1].start()

    def hold(zz, carry):
        rank = rank_tab[y * NZ + zz]
        oarr[y, zz] = obuf[rank]
        larr[y, zz] = lbuf[rank]
        return carry
    lax.fori_loop(0, NZ, hold, 0)
    for copy in back:
        copy.wait_recv()

    def merge(i, carry):
        zz, r = lax.div(i, 2), lax.rem(i, 2)
        prompt = prompt_ref[y * 2 * NZ + i]
        far = jnp.sum(jnp.where(eye, larr[prompt, zz, 0:1], 0.0), axis=1, keepdims=True)
        rows = pl.ds(pl.multiple_of(r * TOK, TOK), TOK)
        near = own_lse[zz, rows]
        top = jnp.maximum(far, near)
        far_w, near_w = jnp.exp2(far - top), jnp.exp2(near - top)
        both = oarr[prompt, zz].astype(F32) * far_w + own_o[zz, rows] * near_w
        abuf[0, pl.ds(pl.multiple_of(i * TOK, TOK), TOK)] = (both / (far_w + near_w)).astype(BF16)
        return carry
    lax.fori_loop(0, 2 * NZ, merge, 0)

    half = LINE // 2

    def a_hop(src, dst, part, way):
        n = {1: 0, 2: 2, 3: 4, 4: 0, 5: 2, 6: 4, 7: 6}[dst] + (part if dst < 7 else 0)
        rows = pl.ds(part * half, half)
        return remote(abuf.at[src, rows], abuf.at[dst, rows], a_s.at[way, n], a_r.at[way, n], left if way else right)

    a_hops = {}
    for part in range(2):
        for dst in range(1, 4):
            a_hops[dst, part] = a_hop(dst - 1, dst, part, 0)
        for dst in range(4, 7):
            a_hops[dst, part] = a_hop(0 if dst == 4 else dst - 1, dst, part, 1)
    a_hops[7, 0] = a_hop(3, 7, 0, 0)
    a_hops[7, 1] = a_hop(6, 7, 1, 1)
    for part in range(2):
        a_hops[1, part].start()
        a_hops[4, part].start()

    for copy in wy:
        copy.wait_recv()

    def project(slots, heads, first=False):
        for slot, head in zip(slots, heads):
            att_ref[:, pl.ds(pl.multiple_of(head * HD, HD), HD)] = abuf[slot, pl.ds(pl.multiple_of(z * OWN, OWN), OWN)]

        def tile(i, carry):
            rows = pl.ds(pl.multiple_of(i * TILE, TILE), TILE)
            a = jnp.concatenate([abuf[slot, rows] for slot in slots], axis=1)
            for yy in range(NY):
                w = jnp.concatenate(
                    [wbuf[yy, pl.ds(pl.multiple_of(head * HD, HD), HD)] for head in heads], axis=0
                )
                term = dot(a, w)
                cols = slice(yy * COLS, (yy + 1) * COLS)
                cacc[rows, cols] = term if first else cacc[rows, cols] + term
            return carry
        lax.fori_loop(0, LINE // TILE, tile, 0)

    project([0], [z], first=True)
    for step in range(1, 4):
        for part in range(2):
            for dst, after in ((step, step + 1 if step < 3 else 7), (step + 3, step + 4)):
                a_hops[dst, part].wait_recv()
                if step < 3 or part == (dst == 6):
                    a_hops[after, part].start()
        project([step, step + 3], [z_at(-step), z_at(step)])
    for part in range(2):
        a_hops[7, part].wait_recv()
    project([7], [z_at(4)])

    csend[...] = cacc[pl.ds(pl.multiple_of(core * half, half), half)].astype(BF16)
    across = remote(csend, crecv, c_s, c_r, (ctx, sibling))
    across.start()
    across.wait_recv()
    for xx in range(NX):
        cols = slice(xx * COLS, (xx + 1) * COLS)
        kept = cacc[pl.ds(pl.multiple_of((1 - core) * half, half), half), cols]
        xsend[xx] = (kept + crecv[:, cols].astype(F32)).astype(BF16)

    xs = []
    for d in range(1, NX):
        to = lax.rem(x + d, NX)
        xs.append(remote(xsend.at[to], xrecv.at[d - 1], x_s.at[d - 1], x_r.at[d - 1], (ctx, to * 2 + core)))
        xs[-1].start()
    for copy in xs:
        copy.wait_recv()
    summed = xsend[x].astype(F32)
    for d in range(NX - 1):
        summed = summed + xrecv[d].astype(F32)
    zsend[...] = summed.astype(BF16).reshape(NZ // 2, OWN, COLS)

    quarter = NZ // 2
    upper, place = lax.div(z, quarter), lax.rem(z, quarter)
    zs = []
    for d in range(quarter):
        to = lax.rem(place + d, quarter)
        zs.append(remote(
            zsend.at[to], zrecv.at[place], z_s.at[d], z_r.at[d], on_line((1 - core) * quarter + to, x * 2 + upper)
        ))
        zs[-1].start()
    for copy in zs:
        copy.wait_recv()
    for i in range(quarter):
        proj_ref[:, i * COLS:(i + 1) * COLS] = zrecv[i]

    for copy in q1 + q2 + wy + back + xs + zs + [across] + list(hops.values()) + list(a_hops.values()):
        copy.wait_send()


def local(queries, resp_keys, resp_values, prefix_keys, prefix_values, prefix_len, prompt_of, out_weight):
    dma = pltpu.SemaphoreType.DMA
    smem, vmem, any_ = pltpu.SMEM, pltpu.VMEM, pl.ANY
    attended, projected = pl.pallas_call(
        kernel,
        out_shape=(
            jax.ShapeDtypeStruct((OWN, NZ * HD), BF16),
            jax.ShapeDtypeStruct((OWN, NX * COLS), BF16),
        ),
        in_specs=[pl.BlockSpec(memory_space=smem)] * 2 + [pl.BlockSpec(memory_space=any_)] * 6,
        out_specs=(pl.BlockSpec(memory_space=vmem), pl.BlockSpec(memory_space=vmem)),
        scratch_shapes=[
            smem((RANKS,), jnp.int32),
            smem((NY * NZ,), jnp.int32),
            vmem((NZ, 2, SLOTS + OWN, HD), BF16),
            vmem((NZ, OWN, HD), BF16),
            vmem((NY - 1, NZ, TOK, HD), BF16),
            vmem((NY * NZ, TOK, HD), BF16),
            vmem((LINE, HD), BF16),
            vmem((LINE, 2 * HD), F32),
            vmem((LINE, HD), F32),
            vmem((NZ, OWN, HD), F32),
            vmem((NZ, OWN, HD), F32),
            vmem((RANKS, TOK, HD), BF16),
            vmem((RANKS, 8, HD), F32),
            vmem((NY - 1, NZ, TOK, HD), BF16),
            vmem((NY - 1, NZ, 8, HD), F32),
            vmem((NY, NZ, TOK, HD), BF16),
            vmem((NY, NZ, 8, HD), F32),
            vmem((NZ, LINE, HD), BF16),
            vmem((NY, NZ * HD, COLS), BF16),
            vmem((LINE, NY * COLS), F32),
            vmem((LINE // 2, NY * COLS), BF16),
            vmem((LINE // 2, NY * COLS), BF16),
            vmem((NX, LINE // 2, COLS), BF16),
            vmem((NX - 1, LINE // 2, COLS), BF16),
            vmem((NZ // 2, OWN, COLS), BF16),
            vmem((NZ // 2, OWN, COLS), BF16),
            dma((6,)),
            dma((NZ - 1,)), dma((NZ - 1,)),
            dma((NY - 1,)), dma((NY - 1,)),
            dma((2, 7)), dma((2, 7)),
            dma((NY - 1,)), dma((NY - 1,)),
            dma((NY - 1,)), dma((NY - 1,)),
            dma((NY - 1,)), dma((NY - 1,)),
            dma((2, 7)), dma((2, 7)),
            dma, dma,
            dma((NX - 1,)), dma((NX - 1,)),
            dma((NZ // 2,)), dma((NZ // 2,)),
        ],
        compiler_params=pltpu.CompilerParams(
            collective_id=0, has_side_effects=True, vmem_limit_bytes=48 * 1024 * 1024
        ),
        cost_estimate=pl.CostEstimate(flops=7_000_000_000, bytes_accessed=3_000_000, transcendentals=9_000_000),
    )(
        prefix_len,
        prompt_of,
        queries.reshape(OWN, NZ * HD),
        resp_keys.reshape(OWN, HD),
        resp_values.reshape(OWN, HD),
        prefix_keys.reshape(SLOTS, HD),
        prefix_values.reshape(SLOTS, HD),
        out_weight,
    )
    return (attended.reshape(2, TOK, 1, NZ * HD), projected)


def solution(mesh):
    in_specs = (
        P("ctx", None, "kvh", None),
        P("ctx", None, "kvh", None),
        P("ctx", None, "kvh", None),
        P("ctx", "kvh", None),
        P("ctx", "kvh", None),
        P(),
        P(),
        P("kvh", "ctx"),
    )
    out_specs = (P("ctx", None, "kvh", None), P("ctx", "kvh"))
    return jax.shard_map(local, mesh=mesh, in_specs=in_specs, out_specs=out_specs, check_vma=False)
```

```python
import math

import jax
import jax.numpy as jnp
from jax import lax
from jax.experimental import pallas as pl
from jax.experimental.pallas import tpu as pltpu
from jax.sharding import PartitionSpec as P

MESH = pl.DeviceIdType.MESH
NY, NZ, NX = 4, 8, 4
TOK, HD, SLOTS = 64, 128, 1024
OWN = 2 * TOK
RANKS = 16
CH, CT = 4, 16
CR = RANKS * CT
COLS = 256
HALF = CR // 2
QUARTER = NZ // 2
PIECE = 2 * CT
MASKED = -1e30
SCALE2 = math.log2(math.e) / math.sqrt(HD)
NT = (((1,), (1,)), ((), ()))
F32, BF16 = jnp.float32, jnp.bfloat16


def dot(a, b):
    return jnp.dot(a, b, preferred_element_type=F32)


def iota(shape, dim):
    return lax.broadcasted_iota(jnp.int32, shape, dim)


def kernel(
    len_in, prompt_in, q_in, rk_in, rv_in, k_in, v_in, w_in,
    att_ref, proj_ref,
    len_ref, prompt_ref, src_tab, rank_tab,
    qall, okv, kv, qline, qsend, qarr, qh, acc, peak, own_o, own_l, own_oarr, own_larr,
    obuf, lbuf, osend, lsend, oarr0, oarr1, oarr2, oarr3, larr0, larr1, larr2, larr3, abuf, wbuf, cbuf, csend, crecv, xsend, xrecv, zsend, zrecv,
    local_s, q1_s, q1_r, q2_s, q2_r, kv_s, kv_r, w_s, w_r, own_s, own_r, o_s, o_r, l_s, l_r, a_s, a_r,
    c_s, c_r, x_s, x_r, z_s, z_r,
):
    ctx, kvh = lax.axis_index("ctx"), lax.axis_index("kvh")
    y, z = lax.div(ctx, NZ), lax.rem(ctx, NZ)
    x, core = lax.div(kvh, 2), lax.rem(kvh, 2)
    upper, place = lax.div(z, QUARTER), lax.rem(z, QUARTER)
    sibling = x * 2 + 1 - core
    started = []
    oarr, larr = (oarr0, oarr1, oarr2, oarr3), (larr0, larr1, larr2, larr3)

    def z_at(d):
        return lax.rem(z + d + NZ, NZ)

    def y_at(d):
        return lax.rem(y + d, NY)

    def on_line(zz, head=None):
        return (y * NZ + zz, kvh if head is None else head)

    def on_column(yy):
        return (yy * NZ + z, kvh)

    def remote(src, dst, ss, rs, dev):
        return pltpu.make_async_remote_copy(
            src_ref=src, dst_ref=dst, send_sem=ss, recv_sem=rs, device_id=dev, device_id_type=MESH
        )

    def start(copy):
        copy.start()
        started.append(copy)
        return copy

    locals_ = [
        pltpu.make_async_copy(src, dst, local_s.at[i])
        for i, (src, dst) in enumerate([
            (k_in, kv.at[0, 0]),
            (v_in, kv.at[0, 1]),
            (q_in, qall),
            (rk_in, okv.at[0]),
            (rv_in, okv.at[1]),
            (w_in, wbuf.at[y]),
            (len_in, len_ref),
            (prompt_in, prompt_ref),
        ])
    ]
    for copy in locals_:
        copy.start()

    barrier = pltpu.get_barrier_semaphore()
    greeted = (
        [on_line(z_at(d)) for d in range(1, NZ)]
        + [on_line(upper * QUARTER + i, sibling) for i in range(QUARTER)]
        + [on_column(y_at(d)) for d in range(1, NY)]
        + [(ctx, lax.rem(x + d, NX) * 2 + core) for d in range(1, NX)]
    )
    for dev in greeted:
        pl.semaphore_signal(barrier, inc=1, device_id=dev, device_id_type=MESH)
    for copy in locals_:
        copy.wait()
    pl.semaphore_wait(barrier, len(greeted))

    def head_cols(head):
        return pl.ds(pl.multiple_of(head * HD, HD), HD)

    q1 = [
        start(remote(
            qall.at[:, head_cols(z_at(d))], qline.at[z], q1_s.at[d - 1], q1_r.at[d - 1], on_line(z_at(d))
        ))
        for d in range(1, NZ)
    ]

    right, left = on_line(z_at(1)), on_line(z_at(-1))

    def slots_of(step, way):
        before = 0 if step == 1 else step - 1 + 3 * way
        return before, 7 if step == 4 else step + 3 * way

    def hop(step, part, way):
        src, dst = slots_of(step, way)
        return remote(
            kv.at[src, part], kv.at[dst, part], kv_s.at[way, part, step - 1], kv_r.at[way, part, step - 1],
            left if way else right,
        )

    hops = {(step, part, way): hop(step, part, way) for step in range(1, 4) for part in range(2) for way in range(2)}
    hops[4, 0, 0] = hop(4, 0, 0)
    hops[4, 1, 1] = hop(4, 1, 1)

    def forward(step, part):
        for way in range(2):
            hops[step, part, way].wait_recv()
            if (step + 1, part, way) in hops:
                start(hops[step + 1, part, way])

    for part in range(2):
        for way in range(2):
            start(hops[1, part, way])

    run = jnp.int32(0)
    through = []
    for s in range(NY * NZ):
        named = (prompt_ref[2 * s] == y) | (prompt_ref[2 * s + 1] == y)
        rank_tab[s] = jnp.minimum(run, RANKS - 1)
        run = run + named.astype(jnp.int32)
        through.append(run)
    for j in range(RANKS):
        src = jnp.int32(0)
        for s in range(NY * NZ):
            src = src + (through[s] <= j).astype(jnp.int32)
        src_tab[j] = jnp.minimum(src, NY * NZ - 1)

    def own_block(head, carry):
        scores = lax.dot_general(qall[:, head_cols(head)], okv[0], NT, preferred_element_type=F32) * SCALE2
        row, col = iota((OWN, OWN), 0), iota((OWN, OWN), 1)
        live = (row >= col) & ((row < TOK) | (col >= TOK))
        scores = jnp.where(live, scores, MASKED)
        top = jnp.max(scores, axis=1, keepdims=True)
        weights = jnp.where(live, jnp.exp2(scores - top), 0.0)
        total = jnp.sum(weights, axis=1, keepdims=True)
        own_o[head] = (dot(weights.astype(BF16), okv[1]) / total).astype(BF16)
        lse = jnp.sum(jnp.where(row == col, top + jnp.log2(total), 0.0), axis=0, keepdims=True)
        own_l[head] = jnp.broadcast_to(lse, (8, HD))
        return carry
    lax.fori_loop(0, NZ, own_block, 0)
    own_oarr[z] = own_o[z]
    own_larr[z] = own_l[z]

    qline[z] = qall[:, head_cols(z)]
    for copy in q1:
        copy.wait_recv()

    def pick(zz, prompt):
        first = prompt_ref[(y * NZ + zz) * 2] == prompt
        return jnp.where(first, qline[zz, 0:TOK], qline[zz, TOK:OWN])

    q2 = []
    for d in range(1, NY):
        def fill(zz, carry, d=d):
            qsend[d - 1, zz] = pick(zz, y_at(d))
            return carry
        lax.fori_loop(0, NZ, fill, 0)
        q2.append(start(remote(
            qsend.at[d - 1], qarr.at[pl.ds(y * NZ, NZ)], q2_s.at[d - 1], q2_r.at[d - 1], on_column(y_at(d))
        )))

    def keep(zz, carry):
        qarr[y * NZ + zz] = pick(zz, y)
        return carry
    lax.fori_loop(0, NZ, keep, 0)

    wy = [
        start(remote(wbuf.at[y], wbuf.at[y], w_s.at[d - 1], w_r.at[d - 1], on_column(y_at(d))))
        for d in range(1, NY)
    ]

    live_len = len_ref[y]
    ones = jnp.ones((SLOTS, HD), BF16)

    def attend(slot, block, chunk, first=False):
        rows = slice(chunk * CR, (chunk + 1) * CR)
        live = block * SLOTS + iota((1, SLOTS), 1) < live_len
        scores = lax.dot_general(qh[rows], kv[slot, 0], NT, preferred_element_type=F32)
        scores = jnp.where(live, scores * SCALE2, MASKED)
        top = jnp.max(scores, axis=1, keepdims=True)
        if not first:
            before = peak[rows]
            top = jnp.maximum(before[:, 0:1], top)
        weights = jnp.exp2(scores - top).astype(BF16)
        mixed = dot(weights, jnp.concatenate([kv[slot, 1], ones], axis=1))
        top = jnp.broadcast_to(top, (CR, HD))
        if not first:
            fade = jnp.exp2(before - top)
            mixed = mixed + acc[rows] * jnp.concatenate([fade, fade], axis=1)
        acc[rows] = mixed
        peak[rows] = top

    def attend_both(step):
        def body(way, carry):
            for chunk in range(CH):
                attend(step + 3 * way, z_at(step * (2 * way - 1)), chunk)
            return carry
        lax.fori_loop(0, 2, body, 0)

    forward(1, 0)
    for copy in q2:
        copy.wait_recv()
    for j in range(RANKS):
        rows = qarr[src_tab[j]]
        for chunk in range(CH):
            qh[chunk * CR + j * CT:chunk * CR + (j + 1) * CT] = rows[chunk * CT:(chunk + 1) * CT]
    for chunk in range(CH):
        attend(0, z, chunk, first=True)
    forward(1, 1)
    attend_both(1)
    forward(2, 0)
    forward(2, 1)
    attend_both(2)
    forward(3, 0)
    forward(3, 1)
    owns = []
    for d in range(1, NZ):
        to = z_at(d)
        owns.append(start(remote(own_o.at[to], own_oarr.at[z], own_s.at[0, d - 1], own_r.at[0, d - 1], on_line(to))))
        owns.append(start(remote(own_l.at[to], own_larr.at[z], own_s.at[1, d - 1], own_r.at[1, d - 1], on_line(to))))
    attend_both(3)
    hops[4, 0, 0].wait_recv()
    hops[4, 1, 1].wait_recv()

    eye = iota((CT, HD), 0) == iota((CT, HD), 1)
    sub = iota((8, HD), 0)

    def finish(chunk):
        first = chunk * CR
        total = acc[first:first + CR, HD:2 * HD]
        out = (acc[first:first + CR, 0:HD] / total).astype(BF16)
        lse = peak[first:first + CR] + jnp.log2(total)
        for j in range(RANKS):
            obuf[chunk, j] = out[j * CT:(j + 1) * CT]
            row = jnp.sum(jnp.where(eye, lse[j * CT:(j + 1) * CT], 0.0), axis=0, keepdims=True)
            lbuf[chunk, j] = jnp.broadcast_to(row, (8, HD))

    back = {}

    def put(chunk, d):
        lines = jnp.zeros((8, HD), F32)
        for zz in range(NZ):
            rank = rank_tab[y_at(d) * NZ + zz]
            lines = jnp.where(sub == zz, lbuf[chunk, rank], lines)
            if d:
                osend[d - 1, chunk, zz] = obuf[chunk, rank]
            else:
                oarr[chunk][y, zz] = obuf[chunk, rank]
        if d:
            lsend[d - 1, chunk] = lines
            to = on_column(y_at(d))
            back[chunk] += [
                start(remote(
                    osend.at[d - 1, chunk], oarr[chunk].at[y], o_s.at[chunk, d - 1], o_r.at[chunk, d - 1], to
                )),
                start(remote(
                    lsend.at[d - 1, chunk], larr[chunk].at[y], l_s.at[chunk, d - 1], l_r.at[chunk, d - 1], to
                )),
            ]
        else:
            larr[chunk][y] = lines

    for chunk in range(CH):
        attend(7, z_at(4), chunk)
        finish(chunk)
        back[chunk] = []
        for d in (2, 1, 3, 0):
            put(chunk, d)

    def merge(chunk):
        for copy in back[chunk]:
            copy.wait_recv()
        for zz in range(NZ):
            for r in range(2):
                prompt = prompt_ref[y * 2 * NZ + zz * 2 + r]
                at = r * TOK + chunk * CT
                far = jnp.sum(jnp.where(eye, larr[chunk][prompt, zz:zz + 1], 0.0), axis=1, keepdims=True)
                here = iota((CT, HD), 0) + at == iota((CT, HD), 1)
                near = jnp.sum(jnp.where(here, own_larr[zz, 0:1], 0.0), axis=1, keepdims=True)
                top = jnp.maximum(far, near)
                far_w, near_w = jnp.exp2(far - top), jnp.exp2(near - top)
                both = oarr[chunk][prompt, zz].astype(F32) * far_w + own_oarr[zz, at:at + CT].astype(F32) * near_w
                row = (zz * 2 + r) * CT
                abuf[0, chunk, row:row + CT] = (both / (far_w + near_w)).astype(BF16)

    def a_hop(chunk, step, way):
        src, dst = slots_of(step, way)
        rows = pl.ds(way * HALF, HALF) if step == 4 else pl.ds(0, CR)
        return remote(
            abuf.at[src, chunk, rows], abuf.at[dst, chunk, rows],
            a_s.at[way, chunk, step - 1], a_r.at[way, chunk, step - 1], left if way else right,
        )

    a_hops = {
        (chunk, step, way): a_hop(chunk, step, way) for chunk in range(CH) for step in range(1, 5) for way in range(2)
    }

    def a_first(chunk):
        for way in range(2):
            start(a_hops[chunk, 1, way])

    def a_forward(chunk, step):
        for way in range(2):
            a_hops[chunk, step, way].wait_recv()
            if step < 4:
                start(a_hops[chunk, step + 1, way])

    heads = [z] + [z_at(-s) for s in range(1, 4)] + [z_at(s) for s in range(1, 5)]
    across, xs, zs = {}, {}, {}

    def product(chunk):
        a_forward(chunk, 4)
        a = jnp.concatenate([abuf[slot, chunk] for slot in range(NZ)], axis=1)
        for yy in range(NY):
            w = jnp.concatenate([wbuf[yy, head_cols(head)] for head in heads], axis=0)
            cbuf[chunk, :, yy * COLS:(yy + 1) * COLS] = dot(a, w)
        csend[chunk] = cbuf[chunk, pl.ds(pl.multiple_of(core * HALF, HALF), HALF)].astype(BF16)
        across[chunk] = start(remote(csend.at[chunk], crecv.at[chunk], c_s.at[chunk], c_r.at[chunk], (ctx, sibling)))
        for slot, head in enumerate(heads):
            for r in range(2):
                rows = pl.ds(pl.multiple_of((z * 2 + r) * CT, CT), CT)
                at = r * TOK + chunk * CT
                att_ref[at:at + CT, head_cols(head)] = abuf[slot, chunk, rows]

    def sum_cores(chunk):
        across[chunk].wait_recv()
        for xx in range(NX):
            cols = slice(xx * COLS, (xx + 1) * COLS)
            kept = cbuf[chunk, pl.ds(pl.multiple_of((1 - core) * HALF, HALF), HALF), cols]
            xsend[chunk, xx] = (kept + crecv[chunk, :, cols].astype(F32)).astype(BF16)
        xs[chunk] = []
        for d in (2, 1, 3):
            to = lax.rem(x + d, NX)
            xs[chunk].append(start(remote(
                xsend.at[chunk, to], xrecv.at[chunk, d - 1], x_s.at[chunk, d - 1], x_r.at[chunk, d - 1],
                (ctx, to * 2 + core),
            )))

    def sum_x(chunk):
        for copy in xs[chunk]:
            copy.wait_recv()
        summed = xsend[chunk, x].astype(F32)
        for d in range(NX - 1):
            summed = summed + xrecv[chunk, d].astype(F32)
        zsend[chunk] = summed.astype(BF16).reshape(QUARTER, PIECE, COLS)
        zs[chunk] = []
        for d in range(QUARTER):
            to = lax.rem(place + d, QUARTER)
            zs[chunk].append(start(remote(
                zsend.at[chunk, to], zrecv.at[chunk, place], z_s.at[chunk, d], z_r.at[chunk, d],
                on_line((1 - core) * QUARTER + to, x * 2 + upper),
            )))

    def deliver(chunk):
        for copy in zs[chunk]:
            copy.wait_recv()
        for i in range(QUARTER):
            for r in range(2):
                at = r * TOK + chunk * CT
                proj_ref[at:at + CT, i * COLS:(i + 1) * COLS] = zrecv[chunk, i, r * CT:(r + 1) * CT]

    for copy in owns:
        copy.wait_recv()
    for chunk in (0, 1):
        merge(chunk)
        a_first(chunk)
    merge(2)
    a_forward(0, 1)
    a_forward(1, 1)
    merge(3)
    for step in (2, 3):
        a_forward(0, step)
        a_forward(1, step)
    a_first(2)
    a_first(3)
    for copy in wy:
        copy.wait_recv()
    product(0)
    product(1)
    a_forward(2, 1)
    a_forward(3, 1)
    sum_cores(0)
    sum_cores(1)
    a_forward(2, 2)
    a_forward(3, 2)
    sum_x(0)
    sum_x(1)
    a_forward(2, 3)
    a_forward(3, 3)
    product(2)
    product(3)
    sum_cores(2)
    sum_cores(3)
    deliver(0)
    deliver(1)
    sum_x(2)
    sum_x(3)
    deliver(2)
    deliver(3)
    for copy in started:
        copy.wait_send()


def local(queries, resp_keys, resp_values, prefix_keys, prefix_values, prefix_len, prompt_of, out_weight):
    dma = pltpu.SemaphoreType.DMA
    smem, vmem, hbm = pltpu.SMEM, pltpu.VMEM, pltpu.HBM
    scratch = [
        smem((NY,), jnp.int32),
        smem((NY * NZ * 2,), jnp.int32),
        smem((RANKS,), jnp.int32),
        smem((NY * NZ,), jnp.int32),
        vmem((OWN, NZ * HD), BF16),
        vmem((2, OWN, HD), BF16),
        vmem((NZ, 2, SLOTS, HD), BF16),
        vmem((NZ, OWN, HD), BF16),
        vmem((NY - 1, NZ, TOK, HD), BF16),
        vmem((NY * NZ, TOK, HD), BF16),
        vmem((CH * CR, HD), BF16),
        vmem((CH * CR, 2 * HD), F32),
        vmem((CH * CR, HD), F32),
        vmem((NZ, OWN, HD), BF16),
        vmem((NZ, 8, HD), F32),
        vmem((NZ, OWN, HD), BF16),
        vmem((NZ, 8, HD), F32),
        vmem((CH, RANKS, CT, HD), BF16),
        vmem((CH, RANKS, 8, HD), F32),
        vmem((NY - 1, CH, NZ, CT, HD), BF16),
        vmem((NY - 1, CH, 8, HD), F32),
        *[vmem((NY, NZ, CT, HD), BF16)] * CH,
        *[vmem((NY, 8, HD), F32)] * CH,
        vmem((NZ, CH, CR, HD), BF16),
        vmem((NY, NZ * HD, COLS), BF16),
        vmem((CH, CR, NY * COLS), F32),
        vmem((CH, HALF, NY * COLS), BF16),
        vmem((CH, HALF, NY * COLS), BF16),
        vmem((CH, NX, HALF, COLS), BF16),
        vmem((CH, NX - 1, HALF, COLS), BF16),
        vmem((CH, QUARTER, PIECE, COLS), BF16),
        vmem((CH, QUARTER, PIECE, COLS), BF16),
        dma((8,)),
    ]
    for shape in (
        (NZ - 1,), (NY - 1,), (2, 2, 4), (NY - 1,), (2, NZ - 1), (CH, NY - 1), (CH, NY - 1), (2, CH, 4),
        (CH,), (CH, NX - 1), (CH, QUARTER),
    ):
        scratch += [dma(shape), dma(shape)]
    attended, projected = pl.pallas_call(
        kernel,
        out_shape=(
            jax.ShapeDtypeStruct((OWN, NZ * HD), BF16),
            jax.ShapeDtypeStruct((OWN, NX * COLS), BF16),
        ),
        in_specs=[pl.BlockSpec(memory_space=hbm)] * 8,
        out_specs=(pl.BlockSpec(memory_space=vmem), pl.BlockSpec(memory_space=vmem)),
        scratch_shapes=scratch,
        compiler_params=pltpu.CompilerParams(
            collective_id=0, has_side_effects=True, vmem_limit_bytes=60 * 1024 * 1024
        ),
        cost_estimate=pl.CostEstimate(flops=7_000_000_000, bytes_accessed=3_000_000, transcendentals=9_000_000),
    )(
        prefix_len,
        prompt_of,
        queries.reshape(OWN, NZ * HD),
        resp_keys.reshape(OWN, HD),
        resp_values.reshape(OWN, HD),
        prefix_keys.reshape(SLOTS, HD),
        prefix_values.reshape(SLOTS, HD),
        out_weight,
    )
    return (attended.reshape(2, TOK, 1, NZ * HD), projected)


def solution(mesh):
    in_specs = (
        P("ctx", None, "kvh", None),
        P("ctx", None, "kvh", None),
        P("ctx", None, "kvh", None),
        P("ctx", "kvh", None),
        P("ctx", "kvh", None),
        P(),
        P(),
        P("kvh", "ctx"),
    )
    out_specs = (P("ctx", None, "kvh", None), P("ctx", "kvh"))
    return jax.shard_map(local, mesh=mesh, in_specs=in_specs, out_specs=out_specs, check_vma=False)
```

```python
import math

import jax
import jax.numpy as jnp
from jax import lax
from jax.experimental import pallas as pl
from jax.experimental.pallas import tpu as pltpu
from jax.sharding import PartitionSpec as P

MESH = pl.DeviceIdType.MESH
NY, NZ, NX = 4, 8, 4
TOK, HD, SLOTS = 64, 128, 1024
OWN = 2 * TOK
RANKS = 16
CH, CT = 4, 16
CR = RANKS * CT
COLS = 256
HALF = CR // 2
QUARTER = NZ // 2
PIECE = 2 * CT
MASKED = -1e30
SCALE2 = math.log2(math.e) / math.sqrt(HD)
NT = (((1,), (1,)), ((), ()))
F32, BF16 = jnp.float32, jnp.bfloat16


def dot(a, b):
    return jnp.dot(a, b, preferred_element_type=F32)


def iota(shape, dim):
    return lax.broadcasted_iota(jnp.int32, shape, dim)


def kernel(
    len_in, prompt_in, q_in, rk_in, rv_in, k_in, v_in, w_in,
    att_ref, proj_ref,
    len_ref, prompt_ref, src_tab, rank_tab,
    qall, okv, kv, qline, qsend, qarr, qh, acc, peak, own_o, own_l, own_oarr, own_larr,
    obuf, lbuf, osend, lsend, oarr0, oarr1, oarr2, oarr3, larr0, larr1, larr2, larr3, abuf, wbuf, cbuf, csend, crecv, xsend, xrecv, zsend, zrecv,
    local_s, q1_s, q1_r, q2_s, q2_r, kv_s, kv_r, w_s, w_r, own_s, own_r, o_s, o_r, l_s, l_r, a_s, a_r,
    c_s, c_r, x_s, x_r, z_s, z_r,
):
    ctx, kvh = lax.axis_index("ctx"), lax.axis_index("kvh")
    y, z = lax.div(ctx, NZ), lax.rem(ctx, NZ)
    x, core = lax.div(kvh, 2), lax.rem(kvh, 2)
    upper, place = lax.div(z, QUARTER), lax.rem(z, QUARTER)
    sibling = x * 2 + 1 - core
    started = []
    oarr, larr = (oarr0, oarr1, oarr2, oarr3), (larr0, larr1, larr2, larr3)

    def z_at(d):
        return lax.rem(z + d + NZ, NZ)

    def y_at(d):
        return lax.rem(y + d, NY)

    def on_line(zz, head=None):
        return (y * NZ + zz, kvh if head is None else head)

    def on_column(yy):
        return (yy * NZ + z, kvh)

    def remote(src, dst, ss, rs, dev):
        return pltpu.make_async_remote_copy(
            src_ref=src, dst_ref=dst, send_sem=ss, recv_sem=rs, device_id=dev, device_id_type=MESH
        )

    def start(copy):
        copy.start()
        started.append(copy)
        return copy

    locals_ = [
        pltpu.make_async_copy(src, dst, local_s.at[i])
        for i, (src, dst) in enumerate([
            (k_in, kv.at[0, 0]),
            (v_in, kv.at[0, 1]),
            (q_in, qall),
            (rk_in, okv.at[0]),
            (rv_in, okv.at[1]),
            (w_in, wbuf.at[y]),
            (len_in, len_ref),
            (prompt_in, prompt_ref),
        ])
    ]
    for copy in locals_:
        copy.start()

    barrier = pltpu.get_barrier_semaphore()
    greeted = (
        [on_line(z_at(d)) for d in range(1, NZ)]
        + [on_line(upper * QUARTER + i, sibling) for i in range(QUARTER)]
        + [on_column(y_at(d)) for d in range(1, NY)]
        + [(ctx, lax.rem(x + d, NX) * 2 + core) for d in range(1, NX)]
    )
    for dev in greeted:
        pl.semaphore_signal(barrier, inc=1, device_id=dev, device_id_type=MESH)
    for copy in locals_:
        copy.wait()
    pl.semaphore_wait(barrier, len(greeted))

    def head_cols(head):
        return pl.ds(pl.multiple_of(head * HD, HD), HD)

    q1 = [
        start(remote(
            qall.at[:, head_cols(z_at(d))], qline.at[z], q1_s.at[d - 1], q1_r.at[d - 1], on_line(z_at(d))
        ))
        for d in range(1, NZ)
    ]

    right, left = on_line(z_at(1)), on_line(z_at(-1))

    def slots_of(step, way):
        before = 0 if step == 1 else step - 1 + 3 * way
        return before, 7 if step == 4 else step + 3 * way

    def hop(step, part, way):
        src, dst = slots_of(step, way)
        return remote(
            kv.at[src, part], kv.at[dst, part], kv_s.at[way, part, step - 1], kv_r.at[way, part, step - 1],
            left if way else right,
        )

    hops = {(step, part, way): hop(step, part, way) for step in range(1, 4) for part in range(2) for way in range(2)}
    hops[4, 0, 0] = hop(4, 0, 0)
    hops[4, 1, 1] = hop(4, 1, 1)

    def forward(step, part):
        for way in range(2):
            hops[step, part, way].wait_recv()
            if (step + 1, part, way) in hops:
                start(hops[step + 1, part, way])

    for part in range(2):
        for way in range(2):
            start(hops[1, part, way])

    run = jnp.int32(0)
    through = []
    for s in range(NY * NZ):
        named = (prompt_ref[2 * s] == y) | (prompt_ref[2 * s + 1] == y)
        rank_tab[s] = jnp.minimum(run, RANKS - 1)
        run = run + named.astype(jnp.int32)
        through.append(run)
    for j in range(RANKS):
        src = jnp.int32(0)
        for s in range(NY * NZ):
            src = src + (through[s] <= j).astype(jnp.int32)
        src_tab[j] = jnp.minimum(src, NY * NZ - 1)

    def own_block(head, carry):
        scores = lax.dot_general(qall[:, head_cols(head)], okv[0], NT, preferred_element_type=F32) * SCALE2
        row, col = iota((OWN, OWN), 0), iota((OWN, OWN), 1)
        live = (row >= col) & ((row < TOK) | (col >= TOK))
        scores = jnp.where(live, scores, MASKED)
        top = jnp.max(scores, axis=1, keepdims=True)
        weights = jnp.where(live, jnp.exp2(scores - top), 0.0)
        total = jnp.sum(weights, axis=1, keepdims=True)
        out = (dot(weights.astype(BF16), okv[1]) / total).astype(BF16)
        for chunk in range(CH):
            for r in range(2):
                at = r * TOK + chunk * CT
                own_o[chunk, head, r * CT:(r + 1) * CT] = out[at:at + CT]
        lse = jnp.sum(jnp.where(row == col, top + jnp.log2(total), 0.0), axis=0, keepdims=True)
        own_l[head] = jnp.broadcast_to(lse, (8, HD))
        return carry
    lax.fori_loop(0, NZ, own_block, 0)
    for chunk in range(CH):
        own_oarr[chunk, z] = own_o[chunk, z]
    own_larr[z] = own_l[z]

    qline[z] = qall[:, head_cols(z)]
    for copy in q1:
        copy.wait_recv()

    def pick(zz, prompt):
        first = prompt_ref[(y * NZ + zz) * 2] == prompt
        return jnp.where(first, qline[zz, 0:TOK], qline[zz, TOK:OWN])

    q2 = []
    for d in range(1, NY):
        def fill(zz, carry, d=d):
            qsend[d - 1, zz] = pick(zz, y_at(d))
            return carry
        lax.fori_loop(0, NZ, fill, 0)
        q2.append(start(remote(
            qsend.at[d - 1], qarr.at[pl.ds(y * NZ, NZ)], q2_s.at[d - 1], q2_r.at[d - 1], on_column(y_at(d))
        )))

    def keep(zz, carry):
        qarr[y * NZ + zz] = pick(zz, y)
        return carry
    lax.fori_loop(0, NZ, keep, 0)

    wy = [
        start(remote(wbuf.at[y], wbuf.at[y], w_s.at[d - 1], w_r.at[d - 1], on_column(y_at(d))))
        for d in range(1, NY)
    ]

    live_len = len_ref[y]
    ones = jnp.ones((SLOTS, HD), BF16)

    def attend(slot, block, chunk, first=False):
        rows = slice(chunk * CR, (chunk + 1) * CR)
        live = block * SLOTS + iota((1, SLOTS), 1) < live_len
        scores = lax.dot_general(qh[rows], kv[slot, 0], NT, preferred_element_type=F32)
        scores = jnp.where(live, scores * SCALE2, MASKED)
        top = jnp.max(scores, axis=1, keepdims=True)
        if not first:
            before = peak[rows]
            top = jnp.maximum(before[:, 0:1], top)
        weights = jnp.exp2(scores - top).astype(BF16)
        mixed = dot(weights, jnp.concatenate([kv[slot, 1], ones], axis=1))
        top = jnp.broadcast_to(top, (CR, HD))
        if not first:
            fade = jnp.exp2(before - top)
            mixed = mixed + acc[rows] * jnp.concatenate([fade, fade], axis=1)
        acc[rows] = mixed
        peak[rows] = top

    def attend_both(step):
        def body(way, carry):
            for chunk in range(CH):
                attend(step + 3 * way, z_at(step * (2 * way - 1)), chunk)
            return carry
        lax.fori_loop(0, 2, body, 0)

    forward(1, 0)
    for copy in q2:
        copy.wait_recv()
    for j in range(RANKS):
        rows = qarr[src_tab[j]]
        for chunk in range(CH):
            qh[chunk * CR + j * CT:chunk * CR + (j + 1) * CT] = rows[chunk * CT:(chunk + 1) * CT]
    for chunk in range(CH):
        attend(0, z, chunk, first=True)
    forward(1, 1)
    attend_both(1)
    forward(2, 0)
    forward(2, 1)
    attend_both(2)
    forward(3, 0)
    forward(3, 1)
    attend_both(3)
    hops[4, 0, 0].wait_recv()
    hops[4, 1, 1].wait_recv()

    eye = iota((CT, HD), 0) == iota((CT, HD), 1)
    sub = iota((8, HD), 0)

    def finish(chunk):
        first = chunk * CR
        total = acc[first:first + CR, HD:2 * HD]
        out = (acc[first:first + CR, 0:HD] / total).astype(BF16)
        lse = peak[first:first + CR] + jnp.log2(total)
        for j in range(RANKS):
            obuf[chunk, j] = out[j * CT:(j + 1) * CT]
            row = jnp.sum(jnp.where(eye, lse[j * CT:(j + 1) * CT], 0.0), axis=0, keepdims=True)
            lbuf[chunk, j] = jnp.broadcast_to(row, (8, HD))

    back = {}

    def put(chunk, d):
        lines = jnp.zeros((8, HD), F32)
        for zz in range(NZ):
            rank = rank_tab[y_at(d) * NZ + zz]
            lines = jnp.where(sub == zz, lbuf[chunk, rank], lines)
            if d:
                osend[d - 1, chunk, zz] = obuf[chunk, rank]
            else:
                oarr[chunk][y, zz] = obuf[chunk, rank]
        if d:
            lsend[d - 1, chunk] = lines
            to = on_column(y_at(d))
            back[chunk] += [
                start(remote(
                    osend.at[d - 1, chunk], oarr[chunk].at[y], o_s.at[chunk, d - 1], o_r.at[chunk, d - 1], to
                )),
                start(remote(
                    lsend.at[d - 1, chunk], larr[chunk].at[y], l_s.at[chunk, d - 1], l_r.at[chunk, d - 1], to
                )),
            ]
        else:
            larr[chunk][y] = lines

    def give(chunk):
        for d in (4, 3, 5, 2, 6, 1, 7):
            to = z_at(d)
            back[chunk].append(start(remote(
                own_o.at[chunk, to], own_oarr.at[chunk, z], own_s.at[chunk, d - 1], own_r.at[chunk, d - 1], on_line(to)
            )))
            if chunk == 0:
                back[chunk].append(start(remote(
                    own_l.at[to], own_larr.at[z], own_s.at[CH, d - 1], own_r.at[CH, d - 1], on_line(to)
                )))

    for chunk in range(CH):
        back[chunk] = []
        give(chunk)
        attend(7, z_at(4), chunk)
        finish(chunk)
        for d in (2, 1, 3, 0):
            put(chunk, d)

    def merge(chunk):
        for copy in back[chunk]:
            copy.wait_recv()
        for zz in range(NZ):
            for r in range(2):
                prompt = prompt_ref[y * 2 * NZ + zz * 2 + r]
                at = r * TOK + chunk * CT
                far = jnp.sum(jnp.where(eye, larr[chunk][prompt, zz:zz + 1], 0.0), axis=1, keepdims=True)
                here = iota((CT, HD), 0) + at == iota((CT, HD), 1)
                near = jnp.sum(jnp.where(here, own_larr[zz, 0:1], 0.0), axis=1, keepdims=True)
                top = jnp.maximum(far, near)
                far_w, near_w = jnp.exp2(far - top), jnp.exp2(near - top)
                both = oarr[chunk][prompt, zz].astype(F32) * far_w + own_oarr[chunk, zz, r * CT:(r + 1) * CT].astype(F32) * near_w
                row = (zz * 2 + r) * CT
                abuf[0, chunk, row:row + CT] = (both / (far_w + near_w)).astype(BF16)

    def a_hop(chunk, step, part, way):
        src, dst = slots_of(step, way)
        rows = pl.ds(part * HALF, HALF)
        return remote(
            abuf.at[src, chunk, rows], abuf.at[dst, chunk, rows],
            a_s.at[way, part, chunk, step - 1], a_r.at[way, part, chunk, step - 1], left if way else right,
        )

    a_hops = {
        (chunk, step, part, way): a_hop(chunk, step, part, way)
        for chunk in range(CH) for step in range(1, 5) for part in range(2) for way in range(2)
        if step < 4 or part == way
    }

    def a_first(chunk):
        for part in range(2):
            for way in range(2):
                start(a_hops[chunk, 1, part, way])

    def a_forward(chunk, step):
        for part in range(2):
            for way in range(2):
                if (chunk, step, part, way) in a_hops:
                    a_hops[chunk, step, part, way].wait_recv()
                if (chunk, step + 1, part, way) in a_hops:
                    start(a_hops[chunk, step + 1, part, way])

    heads = [z] + [z_at(-s) for s in range(1, 4)] + [z_at(s) for s in range(1, 5)]
    across, xs, zs = {}, {}, {}

    def product(chunk):
        a_forward(chunk, 4)
        a = jnp.concatenate([abuf[slot, chunk] for slot in range(NZ)], axis=1)
        for yy in range(NY):
            w = jnp.concatenate([wbuf[yy, head_cols(head)] for head in heads], axis=0)
            cbuf[chunk, :, yy * COLS:(yy + 1) * COLS] = dot(a, w)
        csend[chunk] = cbuf[chunk, pl.ds(pl.multiple_of(core * HALF, HALF), HALF)].astype(BF16)
        across[chunk] = start(remote(csend.at[chunk], crecv.at[chunk], c_s.at[chunk], c_r.at[chunk], (ctx, sibling)))
        for slot, head in enumerate(heads):
            for r in range(2):
                rows = pl.ds(pl.multiple_of((z * 2 + r) * CT, CT), CT)
                at = r * TOK + chunk * CT
                att_ref[at:at + CT, head_cols(head)] = abuf[slot, chunk, rows]

    def sum_cores(chunk):
        across[chunk].wait_recv()
        for xx in range(NX):
            cols = slice(xx * COLS, (xx + 1) * COLS)
            kept = cbuf[chunk, pl.ds(pl.multiple_of((1 - core) * HALF, HALF), HALF), cols]
            xsend[chunk, xx] = (kept + crecv[chunk, :, cols].astype(F32)).astype(BF16)
        xs[chunk] = []
        for d in (2, 1, 3):
            to = lax.rem(x + d, NX)
            xs[chunk].append(start(remote(
                xsend.at[chunk, to], xrecv.at[chunk, d - 1], x_s.at[chunk, d - 1], x_r.at[chunk, d - 1],
                (ctx, to * 2 + core),
            )))

    def sum_x(chunk):
        for copy in xs[chunk]:
            copy.wait_recv()
        summed = xsend[chunk, x].astype(F32)
        for d in range(NX - 1):
            summed = summed + xrecv[chunk, d].astype(F32)
        zsend[chunk] = summed.astype(BF16).reshape(QUARTER, PIECE, COLS)
        zs[chunk] = []
        for d in range(QUARTER):
            to = lax.rem(place + d, QUARTER)
            zs[chunk].append(start(remote(
                zsend.at[chunk, to], zrecv.at[chunk, place], z_s.at[chunk, d], z_r.at[chunk, d],
                on_line((1 - core) * QUARTER + to, x * 2 + upper),
            )))

    def deliver(chunk):
        for copy in zs[chunk]:
            copy.wait_recv()
        for i in range(QUARTER):
            for r in range(2):
                at = r * TOK + chunk * CT
                proj_ref[at:at + CT, i * COLS:(i + 1) * COLS] = zrecv[chunk, i, r * CT:(r + 1) * CT]

    for chunk in (0, 1):
        merge(chunk)
        a_first(chunk)
    a_forward(0, 1)
    merge(2)
    a_forward(1, 1)
    merge(3)
    for step in (2, 3):
        a_forward(0, step)
        a_forward(1, step)
    a_first(2)
    a_first(3)
    for copy in wy:
        copy.wait_recv()
    product(0)
    a_forward(2, 1)
    product(1)
    a_forward(3, 1)
    sum_cores(0)
    a_forward(2, 2)
    sum_cores(1)
    a_forward(3, 2)
    sum_x(0)
    a_forward(2, 3)
    a_forward(3, 3)
    sum_x(1)
    product(2)
    product(3)
    sum_cores(2)
    sum_cores(3)
    deliver(0)
    deliver(1)
    sum_x(2)
    sum_x(3)
    deliver(2)
    deliver(3)
    for copy in started:
        copy.wait_send()


def local(queries, resp_keys, resp_values, prefix_keys, prefix_values, prefix_len, prompt_of, out_weight):
    dma = pltpu.SemaphoreType.DMA
    smem, vmem, hbm = pltpu.SMEM, pltpu.VMEM, pltpu.HBM
    scratch = [
        smem((NY,), jnp.int32),
        smem((NY * NZ * 2,), jnp.int32),
        smem((RANKS,), jnp.int32),
        smem((NY * NZ,), jnp.int32),
        vmem((OWN, NZ * HD), BF16),
        vmem((2, OWN, HD), BF16),
        vmem((NZ, 2, SLOTS, HD), BF16),
        vmem((NZ, OWN, HD), BF16),
        vmem((NY - 1, NZ, TOK, HD), BF16),
        vmem((NY * NZ, TOK, HD), BF16),
        vmem((CH * CR, HD), BF16),
        vmem((CH * CR, 2 * HD), F32),
        vmem((CH * CR, HD), F32),
        vmem((CH, NZ, 2 * CT, HD), BF16),
        vmem((NZ, 8, HD), F32),
        vmem((CH, NZ, 2 * CT, HD), BF16),
        vmem((NZ, 8, HD), F32),
        vmem((CH, RANKS, CT, HD), BF16),
        vmem((CH, RANKS, 8, HD), F32),
        vmem((NY - 1, CH, NZ, CT, HD), BF16),
        vmem((NY - 1, CH, 8, HD), F32),
        *[vmem((NY, NZ, CT, HD), BF16)] * CH,
        *[vmem((NY, 8, HD), F32)] * CH,
        vmem((NZ, CH, CR, HD), BF16),
        vmem((NY, NZ * HD, COLS), BF16),
        vmem((CH, CR, NY * COLS), F32),
        vmem((CH, HALF, NY * COLS), BF16),
        vmem((CH, HALF, NY * COLS), BF16),
        vmem((CH, NX, HALF, COLS), BF16),
        vmem((CH, NX - 1, HALF, COLS), BF16),
        vmem((CH, QUARTER, PIECE, COLS), BF16),
        vmem((CH, QUARTER, PIECE, COLS), BF16),
        dma((8,)),
    ]
    for shape in (
        (NZ - 1,), (NY - 1,), (2, 2, 4), (NY - 1,), (CH + 1, NZ - 1), (CH, NY - 1), (CH, NY - 1), (2, 2, CH, 4),
        (CH,), (CH, NX - 1), (CH, QUARTER),
    ):
        scratch += [dma(shape), dma(shape)]
    attended, projected = pl.pallas_call(
        kernel,
        out_shape=(
            jax.ShapeDtypeStruct((OWN, NZ * HD), BF16),
            jax.ShapeDtypeStruct((OWN, NX * COLS), BF16),
        ),
        in_specs=[pl.BlockSpec(memory_space=hbm)] * 8,
        out_specs=(pl.BlockSpec(memory_space=vmem), pl.BlockSpec(memory_space=vmem)),
        scratch_shapes=scratch,
        compiler_params=pltpu.CompilerParams(
            collective_id=0, has_side_effects=True, vmem_limit_bytes=60 * 1024 * 1024
        ),
        cost_estimate=pl.CostEstimate(flops=7_000_000_000, bytes_accessed=3_000_000, transcendentals=9_000_000),
    )(
        prefix_len,
        prompt_of,
        queries.reshape(OWN, NZ * HD),
        resp_keys.reshape(OWN, HD),
        resp_values.reshape(OWN, HD),
        prefix_keys.reshape(SLOTS, HD),
        prefix_values.reshape(SLOTS, HD),
        out_weight,
    )
    return (attended.reshape(2, TOK, 1, NZ * HD), projected)


def solution(mesh):
    in_specs = (
        P("ctx", None, "kvh", None),
        P("ctx", None, "kvh", None),
        P("ctx", None, "kvh", None),
        P("ctx", "kvh", None),
        P("ctx", "kvh", None),
        P(),
        P(),
        P("kvh", "ctx"),
    )
    out_specs = (P("ctx", None, "kvh", None), P("ctx", "kvh"))
    return jax.shard_map(local, mesh=mesh, in_specs=in_specs, out_specs=out_specs, check_vma=False)
```

```python
import math

import jax
import jax.numpy as jnp
from jax import lax
from jax.experimental import pallas as pl
from jax.experimental.pallas import tpu as pltpu
from jax.sharding import PartitionSpec as P

MESH = pl.DeviceIdType.MESH
NY, NZ, NX = 4, 8, 4
TOK, HD, SLOTS = 64, 128, 1024
OWN = 2 * TOK
RANKS = 16
CH, CT = 4, 16
CR = RANKS * CT
COLS = 256
HALF = CR // 2
QUARTER = NZ // 2
PIECE = 2 * CT
MASKED = -1e30
SCALE2 = math.log2(math.e) / math.sqrt(HD)
NT = (((1,), (1,)), ((), ()))
F32, BF16 = jnp.float32, jnp.bfloat16


def dot(a, b):
    return jnp.dot(a, b, preferred_element_type=F32)


def iota(shape, dim):
    return lax.broadcasted_iota(jnp.int32, shape, dim)


def kernel(
    len_in, prompt_in, q_in, rk_in, rv_in, k_in, v_in, w_in,
    att_ref, proj_ref,
    len_ref, prompt_ref, src_tab, rank_tab,
    qall, okv, kv, qline, qsend, qarr, qh, acc, peak, own_o, own_l, own_oarr, own_larr,
    obuf, lbuf, osend, lsend, oarr0, oarr1, oarr2, oarr3, larr0, larr1, larr2, larr3, abuf, wbuf, cbuf, csend, crecv, xsend, xrecv, zsend, zrecv,
    local_s, q1_s, q1_r, q2_s, q2_r, kv_s, kv_r, w_s, w_r, own_s, own_r, o_s, o_r, l_s, l_r, a_s, a_r,
    c_s, c_r, x_s, x_r, z_s, z_r,
):
    ctx, kvh = lax.axis_index("ctx"), lax.axis_index("kvh")
    y, z = lax.div(ctx, NZ), lax.rem(ctx, NZ)
    x, core = lax.div(kvh, 2), lax.rem(kvh, 2)
    upper, place = lax.div(z, QUARTER), lax.rem(z, QUARTER)
    sibling = x * 2 + 1 - core
    started = []
    oarr, larr = (oarr0, oarr1, oarr2, oarr3), (larr0, larr1, larr2, larr3)

    def z_at(d):
        return lax.rem(z + d + NZ, NZ)

    def y_at(d):
        return lax.rem(y + d, NY)

    def on_line(zz, head=None):
        return (y * NZ + zz, kvh if head is None else head)

    def on_column(yy):
        return (yy * NZ + z, kvh)

    def remote(src, dst, ss, rs, dev):
        return pltpu.make_async_remote_copy(
            src_ref=src, dst_ref=dst, send_sem=ss, recv_sem=rs, device_id=dev, device_id_type=MESH
        )

    def start(copy):
        copy.start()
        started.append(copy)
        return copy

    locals_ = [
        pltpu.make_async_copy(src, dst, local_s.at[i])
        for i, (src, dst) in enumerate([
            (k_in, kv.at[0, 0]),
            (v_in, kv.at[0, 1]),
            (q_in, qall),
            (rk_in, okv.at[0]),
            (rv_in, okv.at[1]),
            (w_in, wbuf.at[y]),
            (len_in, len_ref),
            (prompt_in, prompt_ref),
        ])
    ]
    for copy in locals_:
        copy.start()

    barrier = pltpu.get_barrier_semaphore()
    greeted = (
        [on_line(z_at(d)) for d in range(1, NZ)]
        + [on_line(upper * QUARTER + i, sibling) for i in range(QUARTER)]
        + [on_column(y_at(d)) for d in range(1, NY)]
        + [(ctx, lax.rem(x + d, NX) * 2 + core) for d in range(1, NX)]
    )
    for dev in greeted:
        pl.semaphore_signal(barrier, inc=1, device_id=dev, device_id_type=MESH)
    for copy in locals_:
        copy.wait()
    pl.semaphore_wait(barrier, len(greeted))

    def head_cols(head):
        return pl.ds(pl.multiple_of(head * HD, HD), HD)

    q1 = [
        start(remote(
            qall.at[:, head_cols(z_at(d))], qline.at[z], q1_s.at[d - 1], q1_r.at[d - 1], on_line(z_at(d))
        ))
        for d in range(1, NZ)
    ]

    right, left = on_line(z_at(1)), on_line(z_at(-1))

    def slots_of(step, way):
        before = 0 if step == 1 else step - 1 + 3 * way
        return before, 7 if step == 4 else step + 3 * way

    def hop(step, part, way):
        src, dst = slots_of(step, way)
        return remote(
            kv.at[src, part], kv.at[dst, part], kv_s.at[way, part, step - 1], kv_r.at[way, part, step - 1],
            left if way else right,
        )

    hops = {(step, part, way): hop(step, part, way) for step in range(1, 4) for part in range(2) for way in range(2)}
    hops[4, 0, 0] = hop(4, 0, 0)
    hops[4, 1, 1] = hop(4, 1, 1)

    def forward(step, part):
        for way in range(2):
            hops[step, part, way].wait_recv()
            if (step + 1, part, way) in hops:
                start(hops[step + 1, part, way])

    for part in range(2):
        for way in range(2):
            start(hops[1, part, way])

    run = jnp.int32(0)
    through = []
    for s in range(NY * NZ):
        named = (prompt_ref[2 * s] == y) | (prompt_ref[2 * s + 1] == y)
        rank_tab[s] = jnp.minimum(run, RANKS - 1)
        run = run + named.astype(jnp.int32)
        through.append(run)
    for j in range(RANKS):
        src = jnp.int32(0)
        for s in range(NY * NZ):
            src = src + (through[s] <= j).astype(jnp.int32)
        src_tab[j] = jnp.minimum(src, NY * NZ - 1)

    def own_block(head, carry):
        scores = lax.dot_general(qall[:, head_cols(head)], okv[0], NT, preferred_element_type=F32) * SCALE2
        row, col = iota((OWN, OWN), 0), iota((OWN, OWN), 1)
        live = (row >= col) & ((row < TOK) | (col >= TOK))
        scores = jnp.where(live, scores, MASKED)
        top = jnp.max(scores, axis=1, keepdims=True)
        weights = jnp.where(live, jnp.exp2(scores - top), 0.0)
        total = jnp.sum(weights, axis=1, keepdims=True)
        out = (dot(weights.astype(BF16), okv[1]) / total).astype(BF16)
        for chunk in range(CH):
            for r in range(2):
                at = r * TOK + chunk * CT
                own_o[chunk, head, r * CT:(r + 1) * CT] = out[at:at + CT]
        lse = jnp.sum(jnp.where(row == col, top + jnp.log2(total), 0.0), axis=0, keepdims=True)
        own_l[head] = jnp.broadcast_to(lse, (8, HD))
        return carry
    lax.fori_loop(0, NZ, own_block, 0)
    for chunk in range(CH):
        own_oarr[chunk, z] = own_o[chunk, z]
    own_larr[z] = own_l[z]

    qline[z] = qall[:, head_cols(z)]
    for copy in q1:
        copy.wait_recv()

    def pick(zz, prompt):
        first = prompt_ref[(y * NZ + zz) * 2] == prompt
        return jnp.where(first, qline[zz, 0:TOK], qline[zz, TOK:OWN])

    q2 = []
    for d in range(1, NY):
        def fill(zz, carry, d=d):
            qsend[d - 1, zz] = pick(zz, y_at(d))
            return carry
        lax.fori_loop(0, NZ, fill, 0)
        q2.append(start(remote(
            qsend.at[d - 1], qarr.at[pl.ds(y * NZ, NZ)], q2_s.at[d - 1], q2_r.at[d - 1], on_column(y_at(d))
        )))

    def keep(zz, carry):
        qarr[y * NZ + zz] = pick(zz, y)
        return carry
    lax.fori_loop(0, NZ, keep, 0)

    wy = [
        start(remote(wbuf.at[y], wbuf.at[y], w_s.at[d - 1], w_r.at[d - 1], on_column(y_at(d))))
        for d in range(1, NY)
    ]

    live_len = len_ref[y]
    ones = jnp.ones((SLOTS, HD), BF16)

    def attend(slot, block, chunk, first=False):
        rows = slice(chunk * CR, (chunk + 1) * CR)
        live = block * SLOTS + iota((1, SLOTS), 1) < live_len
        scores = lax.dot_general(qh[rows], kv[slot, 0], NT, preferred_element_type=F32)
        scores = jnp.where(live, scores * SCALE2, MASKED)
        top = jnp.max(scores, axis=1, keepdims=True)
        if not first:
            before = peak[rows]
            top = jnp.maximum(before[:, 0:1], top)
        weights = jnp.exp2(scores - top).astype(BF16)
        mixed = dot(weights, jnp.concatenate([kv[slot, 1], ones], axis=1))
        top = jnp.broadcast_to(top, (CR, HD))
        if not first:
            fade = jnp.exp2(before - top)
            mixed = mixed + acc[rows] * jnp.concatenate([fade, fade], axis=1)
        acc[rows] = mixed
        peak[rows] = top

    def attend_both(step):
        def body(way, carry):
            for chunk in range(CH):
                attend(step + 3 * way, z_at(step * (2 * way - 1)), chunk)
            return carry
        lax.fori_loop(0, 2, body, 0)

    forward(1, 0)
    for copy in q2:
        copy.wait_recv()
    for j in range(RANKS):
        rows = qarr[src_tab[j]]
        for chunk in range(CH):
            qh[chunk * CR + j * CT:chunk * CR + (j + 1) * CT] = rows[chunk * CT:(chunk + 1) * CT]
    for chunk in range(CH):
        attend(0, z, chunk, first=True)
    forward(1, 1)
    attend_both(1)
    forward(2, 0)
    forward(2, 1)
    attend_both(2)
    forward(3, 0)
    forward(3, 1)
    attend_both(3)
    hops[4, 0, 0].wait_recv()
    hops[4, 1, 1].wait_recv()

    eye = iota((CT, HD), 0) == iota((CT, HD), 1)
    sub = iota((8, HD), 0)

    def finish(chunk):
        first = chunk * CR
        total = acc[first:first + CR, HD:2 * HD]
        out = (acc[first:first + CR, 0:HD] / total).astype(BF16)
        lse = peak[first:first + CR] + jnp.log2(total)
        for j in range(RANKS):
            obuf[chunk, j] = out[j * CT:(j + 1) * CT]
            row = jnp.sum(jnp.where(eye, lse[j * CT:(j + 1) * CT], 0.0), axis=0, keepdims=True)
            lbuf[chunk, j] = jnp.broadcast_to(row, (8, HD))

    back = {}

    def put(chunk, d):
        lines = jnp.zeros((8, HD), F32)
        for zz in range(NZ):
            rank = rank_tab[y_at(d) * NZ + zz]
            lines = jnp.where(sub == zz, lbuf[chunk, rank], lines)
            if d:
                osend[d - 1, chunk, zz] = obuf[chunk, rank]
            else:
                oarr[chunk][y, zz] = obuf[chunk, rank]
        if d:
            lsend[d - 1, chunk] = lines
            to = on_column(y_at(d))
            back[chunk] += [
                start(remote(
                    osend.at[d - 1, chunk], oarr[chunk].at[y], o_s.at[chunk, d - 1], o_r.at[chunk, d - 1], to
                )),
                start(remote(
                    lsend.at[d - 1, chunk], larr[chunk].at[y], l_s.at[chunk, d - 1], l_r.at[chunk, d - 1], to
                )),
            ]
        else:
            larr[chunk][y] = lines

    def give(chunk):
        for d in (4, 3, 5, 2, 6, 1, 7):
            to = z_at(d)
            back[chunk].append(start(remote(
                own_o.at[chunk, to], own_oarr.at[chunk, z], own_s.at[chunk, d - 1], own_r.at[chunk, d - 1], on_line(to)
            )))
            if chunk == 0:
                back[chunk].append(start(remote(
                    own_l.at[to], own_larr.at[z], own_s.at[CH, d - 1], own_r.at[CH, d - 1], on_line(to)
                )))

    for chunk in range(CH):
        back[chunk] = []
        give(chunk)
        attend(7, z_at(4), chunk)
        finish(chunk)
        for d in (2, 1, 3, 0):
            put(chunk, d)

    def merge(chunk):
        for copy in back[chunk]:
            copy.wait_recv()
        for zz in range(NZ):
            for r in range(2):
                prompt = prompt_ref[y * 2 * NZ + zz * 2 + r]
                at = r * TOK + chunk * CT
                far = jnp.sum(jnp.where(eye, larr[chunk][prompt, zz:zz + 1], 0.0), axis=1, keepdims=True)
                here = iota((CT, HD), 0) + at == iota((CT, HD), 1)
                near = jnp.sum(jnp.where(here, own_larr[zz, 0:1], 0.0), axis=1, keepdims=True)
                top = jnp.maximum(far, near)
                far_w, near_w = jnp.exp2(far - top), jnp.exp2(near - top)
                both = oarr[chunk][prompt, zz].astype(F32) * far_w + own_oarr[chunk, zz, r * CT:(r + 1) * CT].astype(F32) * near_w
                row = (zz * 2 + r) * CT
                abuf[0, chunk, row:row + CT] = (both / (far_w + near_w)).astype(BF16)

    def a_hop(chunk, step, part, way):
        src, dst = slots_of(step, way)
        rows = pl.ds(part * HALF, HALF)
        return remote(
            abuf.at[src, chunk, rows], abuf.at[dst, chunk, rows],
            a_s.at[way, part, chunk, step - 1], a_r.at[way, part, chunk, step - 1], left if way else right,
        )

    a_hops = {
        (chunk, step, part, way): a_hop(chunk, step, part, way)
        for chunk in range(CH) for step in range(1, 5) for part in range(2) for way in range(2)
        if step < 4 or part == way
    }

    def a_first(chunk):
        for part in range(2):
            for way in range(2):
                start(a_hops[chunk, 1, part, way])

    def a_forward(chunk, step):
        for part in range(2):
            for way in range(2):
                if (chunk, step, part, way) in a_hops:
                    a_hops[chunk, step, part, way].wait_recv()
                if (chunk, step + 1, part, way) in a_hops:
                    start(a_hops[chunk, step + 1, part, way])

    heads = [z] + [z_at(-s) for s in range(1, 4)] + [z_at(s) for s in range(1, 5)]
    across, xs, zs = {}, {}, {}

    def product(chunk):
        a_forward(chunk, 4)
        a = jnp.concatenate([abuf[slot, chunk] for slot in range(NZ)], axis=1)
        for yy in range(NY):
            w = jnp.concatenate([wbuf[yy, head_cols(head)] for head in heads], axis=0)
            cbuf[chunk, :, yy * COLS:(yy + 1) * COLS] = dot(a, w)
        csend[chunk] = cbuf[chunk, pl.ds(pl.multiple_of(core * HALF, HALF), HALF)].astype(BF16)
        across[chunk] = start(remote(csend.at[chunk], crecv.at[chunk], c_s.at[chunk], c_r.at[chunk], (ctx, sibling)))
        for slot, head in enumerate(heads):
            for r in range(2):
                rows = pl.ds(pl.multiple_of((z * 2 + r) * CT, CT), CT)
                at = r * TOK + chunk * CT
                att_ref[at:at + CT, head_cols(head)] = abuf[slot, chunk, rows]

    def sum_cores(chunk):
        across[chunk].wait_recv()
        for xx in range(NX):
            cols = slice(xx * COLS, (xx + 1) * COLS)
            kept = cbuf[chunk, pl.ds(pl.multiple_of((1 - core) * HALF, HALF), HALF), cols]
            xsend[chunk, xx] = (kept + crecv[chunk, :, cols].astype(F32)).astype(BF16)
        xs[chunk] = []
        for d in (2, 1, 3):
            to = lax.rem(x + d, NX)
            xs[chunk].append(start(remote(
                xsend.at[chunk, to], xrecv.at[chunk, d - 1], x_s.at[chunk, d - 1], x_r.at[chunk, d - 1],
                (ctx, to * 2 + core),
            )))

    def sum_x(chunk):
        for copy in xs[chunk]:
            copy.wait_recv()
        summed = xsend[chunk, x].astype(F32)
        for d in range(NX - 1):
            summed = summed + xrecv[chunk, d].astype(F32)
        zsend[chunk] = summed.astype(BF16).reshape(QUARTER, PIECE, COLS)
        zs[chunk] = []
        for d in range(QUARTER):
            to = lax.rem(place + d, QUARTER)
            zs[chunk].append(start(remote(
                zsend.at[chunk, to], zrecv.at[chunk, place], z_s.at[chunk, d], z_r.at[chunk, d],
                on_line((1 - core) * QUARTER + to, x * 2 + upper),
            )))

    def deliver(chunk):
        for copy in zs[chunk]:
            copy.wait_recv()
        for i in range(QUARTER):
            for r in range(2):
                at = r * TOK + chunk * CT
                proj_ref[at:at + CT, i * COLS:(i + 1) * COLS] = zrecv[chunk, i, r * CT:(r + 1) * CT]

    merge(0)
    a_first(0)
    merge(1)
    a_first(1)
    a_forward(0, 1)
    merge(2)
    a_first(2)
    a_forward(1, 1)
    a_forward(0, 2)
    merge(3)
    a_first(3)
    a_forward(2, 1)
    a_forward(1, 2)
    a_forward(0, 3)
    a_forward(3, 1)
    a_forward(2, 2)
    a_forward(1, 3)
    for copy in wy:
        copy.wait_recv()
    product(0)
    a_forward(3, 2)
    a_forward(2, 3)
    sum_cores(0)
    product(1)
    a_forward(3, 3)
    sum_cores(1)
    product(2)
    product(3)
    sum_x(0)
    sum_cores(2)
    sum_x(1)
    sum_cores(3)
    sum_x(2)
    deliver(0)
    deliver(1)
    sum_x(3)
    deliver(2)
    deliver(3)
    for copy in started:
        copy.wait_send()


def local(queries, resp_keys, resp_values, prefix_keys, prefix_values, prefix_len, prompt_of, out_weight):
    dma = pltpu.SemaphoreType.DMA
    smem, vmem, hbm = pltpu.SMEM, pltpu.VMEM, pltpu.HBM
    scratch = [
        smem((NY,), jnp.int32),
        smem((NY * NZ * 2,), jnp.int32),
        smem((RANKS,), jnp.int32),
        smem((NY * NZ,), jnp.int32),
        vmem((OWN, NZ * HD), BF16),
        vmem((2, OWN, HD), BF16),
        vmem((NZ, 2, SLOTS, HD), BF16),
        vmem((NZ, OWN, HD), BF16),
        vmem((NY - 1, NZ, TOK, HD), BF16),
        vmem((NY * NZ, TOK, HD), BF16),
        vmem((CH * CR, HD), BF16),
        vmem((CH * CR, 2 * HD), F32),
        vmem((CH * CR, HD), F32),
        vmem((CH, NZ, 2 * CT, HD), BF16),
        vmem((NZ, 8, HD), F32),
        vmem((CH, NZ, 2 * CT, HD), BF16),
        vmem((NZ, 8, HD), F32),
        vmem((CH, RANKS, CT, HD), BF16),
        vmem((CH, RANKS, 8, HD), F32),
        vmem((NY - 1, CH, NZ, CT, HD), BF16),
        vmem((NY - 1, CH, 8, HD), F32),
        *[vmem((NY, NZ, CT, HD), BF16)] * CH,
        *[vmem((NY, 8, HD), F32)] * CH,
        vmem((NZ, CH, CR, HD), BF16),
        vmem((NY, NZ * HD, COLS), BF16),
        vmem((CH, CR, NY * COLS), F32),
        vmem((CH, HALF, NY * COLS), BF16),
        vmem((CH, HALF, NY * COLS), BF16),
        vmem((CH, NX, HALF, COLS), BF16),
        vmem((CH, NX - 1, HALF, COLS), BF16),
        vmem((CH, QUARTER, PIECE, COLS), BF16),
        vmem((CH, QUARTER, PIECE, COLS), BF16),
        dma((8,)),
    ]
    for shape in (
        (NZ - 1,), (NY - 1,), (2, 2, 4), (NY - 1,), (CH + 1, NZ - 1), (CH, NY - 1), (CH, NY - 1), (2, 2, CH, 4),
        (CH,), (CH, NX - 1), (CH, QUARTER),
    ):
        scratch += [dma(shape), dma(shape)]
    attended, projected = pl.pallas_call(
        kernel,
        out_shape=(
            jax.ShapeDtypeStruct((OWN, NZ * HD), BF16),
            jax.ShapeDtypeStruct((OWN, NX * COLS), BF16),
        ),
        in_specs=[pl.BlockSpec(memory_space=hbm)] * 8,
        out_specs=(pl.BlockSpec(memory_space=vmem), pl.BlockSpec(memory_space=vmem)),
        scratch_shapes=scratch,
        compiler_params=pltpu.CompilerParams(
            collective_id=0, has_side_effects=True, vmem_limit_bytes=60 * 1024 * 1024
        ),
        cost_estimate=pl.CostEstimate(flops=7_000_000_000, bytes_accessed=3_000_000, transcendentals=9_000_000),
    )(
        prefix_len,
        prompt_of,
        queries.reshape(OWN, NZ * HD),
        resp_keys.reshape(OWN, HD),
        resp_values.reshape(OWN, HD),
        prefix_keys.reshape(SLOTS, HD),
        prefix_values.reshape(SLOTS, HD),
        out_weight,
    )
    return (attended.reshape(2, TOK, 1, NZ * HD), projected)


def solution(mesh):
    in_specs = (
        P("ctx", None, "kvh", None),
        P("ctx", None, "kvh", None),
        P("ctx", None, "kvh", None),
        P("ctx", "kvh", None),
        P("ctx", "kvh", None),
        P(),
        P(),
        P("kvh", "ctx"),
    )
    out_specs = (P("ctx", None, "kvh", None), P("ctx", "kvh"))
    return jax.shard_map(local, mesh=mesh, in_specs=in_specs, out_specs=out_specs, check_vma=False)
```

```python
import math

import jax
import jax.numpy as jnp
from jax import lax
from jax.experimental import pallas as pl
from jax.experimental.pallas import tpu as pltpu
from jax.sharding import PartitionSpec as P

MESH = pl.DeviceIdType.MESH
NY, NZ, NX = 4, 8, 4
TOK, HD, SLOTS = 64, 128, 1024
OWN = 2 * TOK
RANKS = 16
CH, CT = 4, 16
CR = RANKS * CT
COLS = 256
HALF = CR // 2
QUARTER = NZ // 2
PIECE = 2 * CT
MASKED = -1e30
SCALE2 = math.log2(math.e) / math.sqrt(HD)
NT = (((1,), (1,)), ((), ()))
F32, BF16 = jnp.float32, jnp.bfloat16


def dot(a, b):
    return jnp.dot(a, b, preferred_element_type=F32)


def iota(shape, dim):
    return lax.broadcasted_iota(jnp.int32, shape, dim)


def kernel(
    len_in, prompt_in, q_in, rk_in, rv_in, k_in, v_in, w_in,
    att_ref, proj_ref,
    len_ref, prompt_ref, src_tab, rank_tab,
    qall, okv, kv, qline, qsend, qarr, qh, acc, peak, own_o, own_l, own_oarr, own_larr,
    obuf, lbuf, osend, lsend, oarr0, oarr1, oarr2, oarr3, larr0, larr1, larr2, larr3, abuf, wbuf, cbuf, csend, crecv, xsend, xrecv, zsend, zrecv,
    local_s, q1_s, q1_r, q2_s, q2_r, kv_s, kv_r, w_s, w_r, own_s, own_r, own_ls, own_lr, o_s, o_r, l_s, l_r, a_s, a_r,
    c_s, c_r, x_s, x_r, z_s, z_r,
):
    ctx, kvh = lax.axis_index("ctx"), lax.axis_index("kvh")
    y, z = lax.div(ctx, NZ), lax.rem(ctx, NZ)
    x, core = lax.div(kvh, 2), lax.rem(kvh, 2)
    upper, place = lax.div(z, QUARTER), lax.rem(z, QUARTER)
    sibling = x * 2 + 1 - core
    oarr, larr = (oarr0, oarr1, oarr2, oarr3), (larr0, larr1, larr2, larr3)

    def z_at(d):
        return lax.rem(z + d + NZ, NZ)

    def y_at(d):
        return lax.rem(y + d, NY)

    def on_line(zz, head=None):
        return (y * NZ + zz, kvh if head is None else head)

    def on_column(yy):
        return (yy * NZ + z, kvh)

    def remote(src, dst, ss, rs, dev):
        return pltpu.make_async_remote_copy(
            src_ref=src, dst_ref=dst, send_sem=ss, recv_sem=rs, device_id=dev, device_id_type=MESH
        )

    def arrived(ref, sem):
        remote(ref, ref, sem, sem, on_line(z_at(1))).wait_recv()

    def sent(ref, sem):
        remote(ref, ref, sem, sem, on_line(z_at(1))).wait_send()

    locals_ = [
        pltpu.make_async_copy(src, dst, local_s.at[i])
        for i, (src, dst) in enumerate([
            (k_in, kv.at[0, 0]),
            (v_in, kv.at[0, 1]),
            (q_in, qall),
            (rk_in, okv.at[0]),
            (rv_in, okv.at[1]),
            (w_in, wbuf.at[y]),
            (len_in, len_ref),
            (prompt_in, prompt_ref),
        ])
    ]
    for copy in locals_:
        copy.start()

    barrier = pltpu.get_barrier_semaphore()
    greeted = (
        [on_line(z_at(d)) for d in range(1, NZ)]
        + [on_line(upper * QUARTER + i, sibling) for i in range(QUARTER)]
        + [on_column(y_at(d)) for d in range(1, NY)]
        + [(ctx, lax.rem(x + d, NX) * 2 + core) for d in range(1, NX)]
    )
    for dev in greeted:
        pl.semaphore_signal(barrier, inc=1, device_id=dev, device_id_type=MESH)
    for copy in locals_:
        copy.wait()
    pl.semaphore_wait(barrier, len(greeted))

    def head_cols(head):
        return pl.ds(pl.multiple_of(head * HD, HD), HD)

    for d in range(1, NZ):
        remote(qall.at[:, head_cols(z_at(d))], qline.at[z], q1_s, q1_r, on_line(z_at(d))).start()

    right, left = on_line(z_at(1)), on_line(z_at(-1))

    def slots_of(step, way):
        before = 0 if step == 1 else step - 1 + 3 * way
        return before, 7 if step == 4 else step + 3 * way

    def hop(step, part, way):
        src, dst = slots_of(step, way)
        rows = pl.ds(way * SLOTS // 2, SLOTS // 2) if step == 4 else pl.ds(0, SLOTS)
        return remote(
            kv.at[src, part, rows], kv.at[dst, part, rows], kv_s, kv_r.at[way, part, step - 1],
            left if way else right,
        )

    hops = {(step, part, way): hop(step, part, way) for step in range(1, 5) for part in range(2) for way in range(2)}

    def forward(step, part):
        for way in range(2):
            hops[step, part, way].wait_recv()
            if step < 4:
                hops[step + 1, part, way].start()

    for part in range(2):
        for way in range(2):
            hops[1, part, way].start()

    run = jnp.int32(0)
    through = []
    for s in range(NY * NZ):
        named = (prompt_ref[2 * s] == y) | (prompt_ref[2 * s + 1] == y)
        rank_tab[s] = jnp.minimum(run, RANKS - 1)
        run = run + named.astype(jnp.int32)
        through.append(run)
    for j in range(RANKS):
        src = jnp.int32(0)
        for s in range(NY * NZ):
            src = src + (through[s] <= j).astype(jnp.int32)
        src_tab[j] = jnp.minimum(src, NY * NZ - 1)

    def own_block(head, carry):
        scores = lax.dot_general(qall[:, head_cols(head)], okv[0], NT, preferred_element_type=F32) * SCALE2
        row, col = iota((OWN, OWN), 0), iota((OWN, OWN), 1)
        live = (row >= col) & ((row < TOK) | (col >= TOK))
        scores = jnp.where(live, scores, MASKED)
        top = jnp.max(scores, axis=1, keepdims=True)
        weights = jnp.where(live, jnp.exp2(scores - top), 0.0)
        total = jnp.sum(weights, axis=1, keepdims=True)
        out = (dot(weights.astype(BF16), okv[1]) / total).astype(BF16)
        for chunk in range(CH):
            for r in range(2):
                at = r * TOK + chunk * CT
                own_o[chunk, head, r * CT:(r + 1) * CT] = out[at:at + CT]
        lse = jnp.sum(jnp.where(row == col, top + jnp.log2(total), 0.0), axis=0, keepdims=True)
        own_l[head] = jnp.broadcast_to(lse, (8, HD))
        return carry
    lax.fori_loop(0, NZ, own_block, 0)
    for chunk in range(CH):
        own_oarr[chunk, z] = own_o[chunk, z]
    own_larr[z] = own_l[z]

    qline[z] = qall[:, head_cols(z)]
    arrived(qline.at[pl.ds(0, NZ - 1)], q1_r)

    def pick(zz, prompt):
        first = prompt_ref[(y * NZ + zz) * 2] == prompt
        return jnp.where(first, qline[zz, 0:TOK], qline[zz, TOK:OWN])

    for d in range(1, NY):
        def fill(zz, carry, d=d):
            qsend[d - 1, zz] = pick(zz, y_at(d))
            return carry
        lax.fori_loop(0, NZ, fill, 0)
        remote(qsend.at[d - 1], qarr.at[pl.ds(y * NZ, NZ)], q2_s, q2_r, on_column(y_at(d))).start()

    def keep(zz, carry):
        qarr[y * NZ + zz] = pick(zz, y)
        return carry
    lax.fori_loop(0, NZ, keep, 0)

    for d in range(1, NY):
        remote(wbuf.at[y], wbuf.at[y], w_s, w_r, on_column(y_at(d))).start()

    live_len = len_ref[y]
    ones = jnp.ones((SLOTS, HD), BF16)

    def attend(slot, block, chunk, first=False):
        rows = slice(chunk * CR, (chunk + 1) * CR)
        live = block * SLOTS + iota((1, SLOTS), 1) < live_len
        scores = lax.dot_general(qh[rows], kv[slot, 0], NT, preferred_element_type=F32)
        scores = jnp.where(live, scores * SCALE2, MASKED)
        top = jnp.max(scores, axis=1, keepdims=True)
        if not first:
            before = peak[rows]
            top = jnp.maximum(before[:, 0:1], top)
        weights = jnp.exp2(scores - top).astype(BF16)
        mixed = dot(weights, jnp.concatenate([kv[slot, 1], ones], axis=1))
        top = jnp.broadcast_to(top, (CR, HD))
        if not first:
            fade = jnp.exp2(before - top)
            mixed = mixed + acc[rows] * jnp.concatenate([fade, fade], axis=1)
        acc[rows] = mixed
        peak[rows] = top

    def attend_both(step):
        def body(way, carry):
            for chunk in range(CH):
                attend(step + 3 * way, z_at(step * (2 * way - 1)), chunk)
            return carry
        lax.fori_loop(0, 2, body, 0)

    forward(1, 0)
    arrived(qarr.at[pl.ds(0, (NY - 1) * NZ)], q2_r)
    for j in range(RANKS):
        rows = qarr[src_tab[j]]
        for chunk in range(CH):
            qh[chunk * CR + j * CT:chunk * CR + (j + 1) * CT] = rows[chunk * CT:(chunk + 1) * CT]
    for chunk in range(CH):
        attend(0, z, chunk, first=True)
    forward(1, 1)
    attend_both(1)
    forward(2, 0)
    forward(2, 1)
    attend_both(2)
    forward(3, 0)
    forward(3, 1)
    attend_both(3)
    forward(4, 0)
    forward(4, 1)

    eye = iota((CT, HD), 0) == iota((CT, HD), 1)
    sub = iota((8, HD), 0)

    def finish(chunk):
        first = chunk * CR
        total = acc[first:first + CR, HD:2 * HD]
        out = (acc[first:first + CR, 0:HD] / total).astype(BF16)
        lse = peak[first:first + CR] + jnp.log2(total)
        for j in range(RANKS):
            obuf[chunk, j] = out[j * CT:(j + 1) * CT]
            row = jnp.sum(jnp.where(eye, lse[j * CT:(j + 1) * CT], 0.0), axis=0, keepdims=True)
            lbuf[chunk, j] = jnp.broadcast_to(row, (8, HD))

    def put(chunk, d):
        lines = jnp.zeros((8, HD), F32)
        for zz in range(NZ):
            rank = rank_tab[y_at(d) * NZ + zz]
            lines = jnp.where(sub == zz, lbuf[chunk, rank], lines)
            if d:
                osend[d - 1, chunk, zz] = obuf[chunk, rank]
            else:
                oarr[chunk][y, zz] = obuf[chunk, rank]
        if d:
            lsend[d - 1, chunk] = lines
            to = on_column(y_at(d))
            remote(osend.at[d - 1, chunk], oarr[chunk].at[y], o_s, o_r.at[chunk], to).start()
            remote(lsend.at[d - 1, chunk], larr[chunk].at[y], l_s, l_r.at[chunk], to).start()
        else:
            larr[chunk][y] = lines

    def give(chunk):
        for d in (4, 3, 5, 2, 6, 1, 7):
            to = z_at(d)
            remote(own_o.at[chunk, to], own_oarr.at[chunk, z], own_s, own_r.at[chunk], on_line(to)).start()
            if chunk == 0:
                remote(own_l.at[to], own_larr.at[z], own_ls, own_lr, on_line(to)).start()

    for chunk in range(CH):
        give(chunk)
        attend(7, z_at(4), chunk)
        finish(chunk)
        for d in (2, 1, 3, 0):
            put(chunk, d)

    def merge(chunk):
        arrived(own_oarr.at[chunk, pl.ds(0, NZ - 1)], own_r.at[chunk])
        if chunk == 0:
            arrived(own_larr.at[pl.ds(0, NZ - 1)], own_lr)
        arrived(oarr[chunk].at[pl.ds(0, NY - 1)], o_r.at[chunk])
        arrived(larr[chunk].at[pl.ds(0, NY - 1)], l_r.at[chunk])
        for zz in range(NZ):
            for r in range(2):
                prompt = prompt_ref[y * 2 * NZ + zz * 2 + r]
                at = r * TOK + chunk * CT
                far = jnp.sum(jnp.where(eye, larr[chunk][prompt, zz:zz + 1], 0.0), axis=1, keepdims=True)
                here = iota((CT, HD), 0) + at == iota((CT, HD), 1)
                near = jnp.sum(jnp.where(here, own_larr[zz, 0:1], 0.0), axis=1, keepdims=True)
                top = jnp.maximum(far, near)
                far_w, near_w = jnp.exp2(far - top), jnp.exp2(near - top)
                both = oarr[chunk][prompt, zz].astype(F32) * far_w + own_oarr[chunk, zz, r * CT:(r + 1) * CT].astype(F32) * near_w
                row = (zz * 2 + r) * CT
                abuf[0, chunk, row:row + CT] = (both / (far_w + near_w)).astype(BF16)

    def a_hop(chunk, step, part, way):
        src, dst = slots_of(step, way)
        rows = pl.ds(part * HALF, HALF)
        return remote(
            abuf.at[src, chunk, rows], abuf.at[dst, chunk, rows],
            a_s, a_r.at[way, part, chunk, step - 1], left if way else right,
        )

    a_hops = {
        (chunk, step, part, way): a_hop(chunk, step, part, way)
        for chunk in range(CH) for step in range(1, 5) for part in range(2) for way in range(2)
        if step < 4 or part == way
    }

    def a_first(chunk):
        for part in range(2):
            for way in range(2):
                a_hops[chunk, 1, part, way].start()

    def a_forward(chunk, step):
        for part in range(2):
            for way in range(2):
                if (chunk, step, part, way) in a_hops:
                    a_hops[chunk, step, part, way].wait_recv()
                if (chunk, step + 1, part, way) in a_hops:
                    a_hops[chunk, step + 1, part, way].start()

    heads = [z] + [z_at(-s) for s in range(1, 4)] + [z_at(s) for s in range(1, 5)]

    def product(chunk):
        a_forward(chunk, 4)
        a = jnp.concatenate([abuf[slot, chunk] for slot in range(NZ)], axis=1)
        for yy in range(NY):
            w = jnp.concatenate([wbuf[yy, head_cols(head)] for head in heads], axis=0)
            cbuf[chunk, :, yy * COLS:(yy + 1) * COLS] = dot(a, w)
        csend[chunk] = cbuf[chunk, pl.ds(pl.multiple_of(core * HALF, HALF), HALF)].astype(BF16)
        remote(csend.at[chunk], crecv.at[chunk], c_s, c_r.at[chunk], (ctx, sibling)).start()
        for slot, head in enumerate(heads):
            for r in range(2):
                rows = pl.ds(pl.multiple_of((z * 2 + r) * CT, CT), CT)
                at = r * TOK + chunk * CT
                att_ref[at:at + CT, head_cols(head)] = abuf[slot, chunk, rows]

    def sum_cores(chunk):
        arrived(crecv.at[chunk], c_r.at[chunk])
        for xx in range(NX):
            cols = slice(xx * COLS, (xx + 1) * COLS)
            kept = cbuf[chunk, pl.ds(pl.multiple_of((1 - core) * HALF, HALF), HALF), cols]
            xsend[chunk, xx] = (kept + crecv[chunk, :, cols].astype(F32)).astype(BF16)
        for d in (2, 1, 3):
            to = lax.rem(x + d, NX)
            remote(xsend.at[chunk, to], xrecv.at[chunk, d - 1], x_s, x_r.at[chunk], (ctx, to * 2 + core)).start()

    def sum_x(chunk):
        arrived(xrecv.at[chunk], x_r.at[chunk])
        summed = xsend[chunk, x].astype(F32)
        for d in range(NX - 1):
            summed = summed + xrecv[chunk, d].astype(F32)
        zsend[chunk] = summed.astype(BF16).reshape(QUARTER, PIECE, COLS)
        for d in range(QUARTER):
            to = lax.rem(place + d, QUARTER)
            remote(
                zsend.at[chunk, to], zrecv.at[chunk, place], z_s, z_r.at[chunk],
                on_line((1 - core) * QUARTER + to, x * 2 + upper),
            ).start()

    def deliver(chunk):
        arrived(zrecv.at[chunk], z_r.at[chunk])
        for i in range(QUARTER):
            for r in range(2):
                at = r * TOK + chunk * CT
                proj_ref[at:at + CT, i * COLS:(i + 1) * COLS] = zrecv[chunk, i, r * CT:(r + 1) * CT]

    merge(0)
    a_first(0)
    merge(1)
    a_first(1)
    a_forward(0, 1)
    merge(2)
    a_first(2)
    a_forward(1, 1)
    a_forward(0, 2)
    merge(3)
    a_first(3)
    a_forward(2, 1)
    a_forward(1, 2)
    a_forward(0, 3)
    a_forward(3, 1)
    a_forward(2, 2)
    a_forward(1, 3)
    arrived(wbuf.at[pl.ds(0, NY - 1)], w_r)
    product(0)
    a_forward(3, 2)
    a_forward(2, 3)
    sum_cores(0)
    product(1)
    a_forward(3, 3)
    sum_cores(1)
    product(2)
    sum_x(0)
    product(3)
    sum_cores(2)
    sum_x(1)
    sum_cores(3)
    sum_x(2)
    sum_x(3)
    deliver(0)
    deliver(1)
    deliver(2)
    deliver(3)
    sent(qline.at[pl.ds(0, NZ - 1)], q1_s)
    sent(qsend, q2_s)
    sent(wbuf.at[pl.ds(0, NY - 1)], w_s)
    sent(own_o.at[:, pl.ds(0, NZ - 1)], own_s)
    sent(own_l.at[pl.ds(0, NZ - 1)], own_ls)
    sent(osend, o_s)
    sent(lsend, l_s)
    sent(kv.at[pl.ds(0, NZ - 1)], kv_s)
    sent(abuf.at[pl.ds(0, NZ - 1)], a_s)
    sent(csend, c_s)
    sent(xrecv, x_s)
    sent(zsend, z_s)


def local(queries, resp_keys, resp_values, prefix_keys, prefix_values, prefix_len, prompt_of, out_weight):
    dma = pltpu.SemaphoreType.DMA
    smem, vmem, hbm = pltpu.SMEM, pltpu.VMEM, pltpu.HBM
    scratch = [
        smem((NY,), jnp.int32),
        smem((NY * NZ * 2,), jnp.int32),
        smem((RANKS,), jnp.int32),
        smem((NY * NZ,), jnp.int32),
        vmem((OWN, NZ * HD), BF16),
        vmem((2, OWN, HD), BF16),
        vmem((NZ, 2, SLOTS, HD), BF16),
        vmem((NZ, OWN, HD), BF16),
        vmem((NY - 1, NZ, TOK, HD), BF16),
        vmem((NY * NZ, TOK, HD), BF16),
        vmem((CH * CR, HD), BF16),
        vmem((CH * CR, 2 * HD), F32),
        vmem((CH * CR, HD), F32),
        vmem((CH, NZ, 2 * CT, HD), BF16),
        vmem((NZ, 8, HD), F32),
        vmem((CH, NZ, 2 * CT, HD), BF16),
        vmem((NZ, 8, HD), F32),
        vmem((CH, RANKS, CT, HD), BF16),
        vmem((CH, RANKS, 8, HD), F32),
        vmem((NY - 1, CH, NZ, CT, HD), BF16),
        vmem((NY - 1, CH, 8, HD), F32),
        *[vmem((NY, NZ, CT, HD), BF16)] * CH,
        *[vmem((NY, 8, HD), F32)] * CH,
        vmem((NZ, CH, CR, HD), BF16),
        vmem((NY, NZ * HD, COLS), BF16),
        vmem((CH, CR, NY * COLS), F32),
        vmem((CH, HALF, NY * COLS), BF16),
        vmem((CH, HALF, NY * COLS), BF16),
        vmem((CH, NX, HALF, COLS), BF16),
        vmem((CH, NX - 1, HALF, COLS), BF16),
        vmem((CH, QUARTER, PIECE, COLS), BF16),
        vmem((CH, QUARTER, PIECE, COLS), BF16),
        dma((8,)),
    ]
    for shape in ((), (), (2, 2, 4), (), (CH,), (), (CH,), (CH,), (2, 2, CH, 4), (CH,), (CH,), (CH,)):
        scratch += [dma, dma(shape) if shape else dma]
    attended, projected = pl.pallas_call(
        kernel,
        out_shape=(
            jax.ShapeDtypeStruct((OWN, NZ * HD), BF16),
            jax.ShapeDtypeStruct((OWN, NX * COLS), BF16),
        ),
        in_specs=[pl.BlockSpec(memory_space=hbm)] * 8,
        out_specs=(pl.BlockSpec(memory_space=vmem), pl.BlockSpec(memory_space=vmem)),
        scratch_shapes=scratch,
        compiler_params=pltpu.CompilerParams(
            collective_id=0, has_side_effects=True, vmem_limit_bytes=60 * 1024 * 1024
        ),
        cost_estimate=pl.CostEstimate(flops=7_000_000_000, bytes_accessed=3_000_000, transcendentals=9_000_000),
    )(
        prefix_len,
        prompt_of,
        queries.reshape(OWN, NZ * HD),
        resp_keys.reshape(OWN, HD),
        resp_values.reshape(OWN, HD),
        prefix_keys.reshape(SLOTS, HD),
        prefix_values.reshape(SLOTS, HD),
        out_weight,
    )
    return (attended.reshape(2, TOK, 1, NZ * HD), projected)


def solution(mesh):
    in_specs = (
        P("ctx", None, "kvh", None),
        P("ctx", None, "kvh", None),
        P("ctx", None, "kvh", None),
        P("ctx", "kvh", None),
        P("ctx", "kvh", None),
        P(),
        P(),
        P("kvh", "ctx"),
    )
    out_specs = (P("ctx", None, "kvh", None), P("ctx", "kvh"))
    return jax.shard_map(local, mesh=mesh, in_specs=in_specs, out_specs=out_specs, check_vma=False)
```

```python
import math

import jax
import jax.numpy as jnp
from jax import lax
from jax.experimental import pallas as pl
from jax.experimental.pallas import tpu as pltpu
from jax.sharding import PartitionSpec as P

MESH = pl.DeviceIdType.MESH
NY, NZ, NX = 4, 8, 4
TOK, HD, SLOTS = 64, 128, 1024
OWN = 2 * TOK
RANKS = 16
CH, CT = 4, 16
CR = RANKS * CT
UNITS = 2 * CH
UR = NZ * CT
COLS = 256
HALF = UR // 2
QUARTER = NZ // 2
PIECE = CT
MASKED = -1e30
SCALE2 = math.log2(math.e) / math.sqrt(HD)
NT = (((1,), (1,)), ((), ()))
F32, BF16 = jnp.float32, jnp.bfloat16


def dot(a, b):
    return jnp.dot(a, b, preferred_element_type=F32)


def iota(shape, dim):
    return lax.broadcasted_iota(jnp.int32, shape, dim)


def kernel(
    len_in, prompt_in, q_in, rk_in, rv_in, k_in, v_in, w_in,
    att_ref, proj_ref,
    len_ref, prompt_ref, src_tab, rank_tab,
    qall, okv, kv, qline, qsend, qarr, qh, acc, peak, own_o, own_l, own_oarr, own_larr,
    obuf, lbuf, osend, lsend, oarr0, oarr1, oarr2, oarr3, larr0, larr1, larr2, larr3, abuf, wbuf, cbuf, csend, crecv, xsend, xrecv, zsend, zrecv,
    local_s, q1_s, q1_r, q2_s, q2_r, kv_s, kv_r, w_s, w_r, own_s, own_r, own_ls, own_lr, o_s, o_r, l_s, l_r, a_s, a_r,
    c_s, c_r, x_s, x_r, z_s, z_r,
):
    ctx, kvh = lax.axis_index("ctx"), lax.axis_index("kvh")
    y, z = lax.div(ctx, NZ), lax.rem(ctx, NZ)
    x, core = lax.div(kvh, 2), lax.rem(kvh, 2)
    upper, place = lax.div(z, QUARTER), lax.rem(z, QUARTER)
    sibling = x * 2 + 1 - core
    oarr, larr = (oarr0, oarr1, oarr2, oarr3), (larr0, larr1, larr2, larr3)

    def z_at(d):
        return lax.rem(z + d + NZ, NZ)

    def y_at(d):
        return lax.rem(y + d, NY)

    def on_line(zz, head=None):
        return (y * NZ + zz, kvh if head is None else head)

    def on_column(yy):
        return (yy * NZ + z, kvh)

    def remote(src, dst, ss, rs, dev):
        return pltpu.make_async_remote_copy(
            src_ref=src, dst_ref=dst, send_sem=ss, recv_sem=rs, device_id=dev, device_id_type=MESH
        )

    def arrived(ref, sem):
        remote(ref, ref, sem, sem, on_line(z_at(1))).wait_recv()

    def sent(ref, sem):
        remote(ref, ref, sem, sem, on_line(z_at(1))).wait_send()

    locals_ = [
        pltpu.make_async_copy(src, dst, local_s.at[i])
        for i, (src, dst) in enumerate([
            (k_in, kv.at[0, 0]),
            (v_in, kv.at[0, 1]),
            (q_in, qall),
            (rk_in, okv.at[0]),
            (rv_in, okv.at[1]),
            (w_in, wbuf.at[y]),
            (len_in, len_ref),
            (prompt_in, prompt_ref),
        ])
    ]
    for copy in locals_:
        copy.start()

    barrier = pltpu.get_barrier_semaphore()
    greeted = (
        [on_line(z_at(d)) for d in range(1, NZ)]
        + [on_line(upper * QUARTER + i, sibling) for i in range(QUARTER)]
        + [on_column(y_at(d)) for d in range(1, NY)]
        + [(ctx, lax.rem(x + d, NX) * 2 + core) for d in range(1, NX)]
    )
    for dev in greeted:
        pl.semaphore_signal(barrier, inc=1, device_id=dev, device_id_type=MESH)
    for copy in locals_:
        copy.wait()
    pl.semaphore_wait(barrier, len(greeted))

    def head_cols(head):
        return pl.ds(pl.multiple_of(head * HD, HD), HD)

    for d in range(1, NZ):
        remote(qall.at[:, head_cols(z_at(d))], qline.at[z], q1_s, q1_r, on_line(z_at(d))).start()

    right, left = on_line(z_at(1)), on_line(z_at(-1))

    def slots_of(step, way):
        before = 0 if step == 1 else step - 1 + 3 * way
        return before, 7 if step == 4 else step + 3 * way

    def hop(step, part, way):
        src, dst = slots_of(step, way)
        rows = pl.ds(way * SLOTS // 2, SLOTS // 2) if step == 4 else pl.ds(0, SLOTS)
        return remote(
            kv.at[src, part, rows], kv.at[dst, part, rows], kv_s, kv_r.at[way, part, step - 1],
            left if way else right,
        )

    hops = {(step, part, way): hop(step, part, way) for step in range(1, 5) for part in range(2) for way in range(2)}

    def forward(step, part):
        for way in range(2):
            hops[step, part, way].wait_recv()
            if step < 4:
                hops[step + 1, part, way].start()

    for part in range(2):
        for way in range(2):
            hops[1, part, way].start()

    run = jnp.int32(0)
    through = []
    for s in range(NY * NZ):
        named = (prompt_ref[2 * s] == y) | (prompt_ref[2 * s + 1] == y)
        rank_tab[s] = jnp.minimum(run, RANKS - 1)
        run = run + named.astype(jnp.int32)
        through.append(run)
    for j in range(RANKS):
        src = jnp.int32(0)
        for s in range(NY * NZ):
            src = src + (through[s] <= j).astype(jnp.int32)
        src_tab[j] = jnp.minimum(src, NY * NZ - 1)

    def own_block(head, carry):
        scores = lax.dot_general(qall[:, head_cols(head)], okv[0], NT, preferred_element_type=F32) * SCALE2
        row, col = iota((OWN, OWN), 0), iota((OWN, OWN), 1)
        live = (row >= col) & ((row < TOK) | (col >= TOK))
        scores = jnp.where(live, scores, MASKED)
        top = jnp.max(scores, axis=1, keepdims=True)
        weights = jnp.where(live, jnp.exp2(scores - top), 0.0)
        total = jnp.sum(weights, axis=1, keepdims=True)
        out = (dot(weights.astype(BF16), okv[1]) / total).astype(BF16)
        for chunk in range(CH):
            for r in range(2):
                at = r * TOK + chunk * CT
                own_o[chunk, head, r * CT:(r + 1) * CT] = out[at:at + CT]
        lse = jnp.sum(jnp.where(row == col, top + jnp.log2(total), 0.0), axis=0, keepdims=True)
        own_l[head] = jnp.broadcast_to(lse, (8, HD))
        return carry
    lax.fori_loop(0, NZ, own_block, 0)
    for chunk in range(CH):
        own_oarr[chunk, z] = own_o[chunk, z]
    own_larr[z] = own_l[z]

    qline[z] = qall[:, head_cols(z)]
    arrived(qline.at[pl.ds(0, NZ - 1)], q1_r)

    def pick(zz, prompt):
        first = prompt_ref[(y * NZ + zz) * 2] == prompt
        return jnp.where(first, qline[zz, 0:TOK], qline[zz, TOK:OWN])

    for d in range(1, NY):
        def fill(zz, carry, d=d):
            qsend[d - 1, zz] = pick(zz, y_at(d))
            return carry
        lax.fori_loop(0, NZ, fill, 0)
        remote(qsend.at[d - 1], qarr.at[pl.ds(y * NZ, NZ)], q2_s, q2_r, on_column(y_at(d))).start()

    def keep(zz, carry):
        qarr[y * NZ + zz] = pick(zz, y)
        return carry
    lax.fori_loop(0, NZ, keep, 0)

    for d in range(1, NY):
        remote(wbuf.at[y], wbuf.at[y], w_s, w_r, on_column(y_at(d))).start()

    live_len = len_ref[y]
    ones = jnp.ones((SLOTS, HD), BF16)

    def attend(slot, block, chunk, first=False):
        rows = slice(chunk * CR, (chunk + 1) * CR)
        live = block * SLOTS + iota((1, SLOTS), 1) < live_len
        scores = lax.dot_general(qh[rows], kv[slot, 0], NT, preferred_element_type=F32)
        scores = jnp.where(live, scores * SCALE2, MASKED)
        top = jnp.max(scores, axis=1, keepdims=True)
        if not first:
            before = peak[rows]
            top = jnp.maximum(before[:, 0:1], top)
        weights = jnp.exp2(scores - top).astype(BF16)
        mixed = dot(weights, jnp.concatenate([kv[slot, 1], ones], axis=1))
        top = jnp.broadcast_to(top, (CR, HD))
        if not first:
            fade = jnp.exp2(before - top)
            mixed = mixed + acc[rows] * jnp.concatenate([fade, fade], axis=1)
        acc[rows] = mixed
        peak[rows] = top

    def attend_both(step):
        def body(way, carry):
            for chunk in range(CH):
                attend(step + 3 * way, z_at(step * (2 * way - 1)), chunk)
            return carry
        lax.fori_loop(0, 2, body, 0)

    forward(1, 0)
    arrived(qarr.at[pl.ds(0, (NY - 1) * NZ)], q2_r)
    for j in range(RANKS):
        rows = qarr[src_tab[j]]
        for chunk in range(CH):
            qh[chunk * CR + j * CT:chunk * CR + (j + 1) * CT] = rows[chunk * CT:(chunk + 1) * CT]
    for chunk in range(CH):
        attend(0, z, chunk, first=True)
    forward(1, 1)
    attend_both(1)
    forward(2, 0)
    forward(2, 1)
    attend_both(2)
    forward(3, 0)
    forward(3, 1)
    attend_both(3)
    forward(4, 0)
    forward(4, 1)

    eye = iota((CT, HD), 0) == iota((CT, HD), 1)
    sub = iota((8, HD), 0)

    def finish(chunk):
        first = chunk * CR
        total = acc[first:first + CR, HD:2 * HD]
        out = (acc[first:first + CR, 0:HD] / total).astype(BF16)
        lse = peak[first:first + CR] + jnp.log2(total)
        for j in range(RANKS):
            obuf[chunk, j] = out[j * CT:(j + 1) * CT]
            row = jnp.sum(jnp.where(eye, lse[j * CT:(j + 1) * CT], 0.0), axis=0, keepdims=True)
            lbuf[chunk, j] = jnp.broadcast_to(row, (8, HD))

    def put(chunk, d):
        lines = jnp.zeros((8, HD), F32)
        for zz in range(NZ):
            rank = rank_tab[y_at(d) * NZ + zz]
            lines = jnp.where(sub == zz, lbuf[chunk, rank], lines)
            if d:
                osend[d - 1, chunk, zz] = obuf[chunk, rank]
            else:
                oarr[chunk][y, zz] = obuf[chunk, rank]
        if d:
            lsend[d - 1, chunk] = lines
            to = on_column(y_at(d))
            remote(osend.at[d - 1, chunk], oarr[chunk].at[y], o_s, o_r.at[chunk], to).start()
            remote(lsend.at[d - 1, chunk], larr[chunk].at[y], l_s, l_r.at[chunk], to).start()
        else:
            larr[chunk][y] = lines

    def give(chunk):
        for d in (4, 3, 5, 2, 6, 1, 7):
            to = z_at(d)
            remote(own_o.at[chunk, to], own_oarr.at[chunk, z], own_s, own_r.at[chunk], on_line(to)).start()
            if chunk == 0:
                remote(own_l.at[to], own_larr.at[z], own_ls, own_lr, on_line(to)).start()

    for chunk in range(CH):
        give(chunk)
        attend(7, z_at(4), chunk)
        finish(chunk)
        for d in (2, 1, 3, 0):
            put(chunk, d)

    def merge(chunk):
        arrived(own_oarr.at[chunk, pl.ds(0, NZ - 1)], own_r.at[chunk])
        if chunk == 0:
            arrived(own_larr.at[pl.ds(0, NZ - 1)], own_lr)
        arrived(oarr[chunk].at[pl.ds(0, NY - 1)], o_r.at[chunk])
        arrived(larr[chunk].at[pl.ds(0, NY - 1)], l_r.at[chunk])
        for zz in range(NZ):
            for r in range(2):
                prompt = prompt_ref[y * 2 * NZ + zz * 2 + r]
                at = r * TOK + chunk * CT
                far = jnp.sum(jnp.where(eye, larr[chunk][prompt, zz:zz + 1], 0.0), axis=1, keepdims=True)
                here = iota((CT, HD), 0) + at == iota((CT, HD), 1)
                near = jnp.sum(jnp.where(here, own_larr[zz, 0:1], 0.0), axis=1, keepdims=True)
                top = jnp.maximum(far, near)
                far_w, near_w = jnp.exp2(far - top), jnp.exp2(near - top)
                both = oarr[chunk][prompt, zz].astype(F32) * far_w + own_oarr[chunk, zz, r * CT:(r + 1) * CT].astype(F32) * near_w
                abuf[0, 2 * chunk + r, zz * CT:(zz + 1) * CT] = (both / (far_w + near_w)).astype(BF16)

    def a_hop(chunk, step, way):
        src, dst = slots_of(step, way)
        rows = pl.ds(way * HALF, HALF) if step == 4 else pl.ds(0, UR)
        return remote(
            abuf.at[src, chunk, rows], abuf.at[dst, chunk, rows],
            a_s, a_r.at[way, chunk, step - 1], left if way else right,
        )

    a_hops = {
        (chunk, step, way): a_hop(chunk, step, way) for chunk in range(UNITS) for step in range(1, 5) for way in range(2)
    }

    def a_first(chunk):
        for way in range(2):
            a_hops[chunk, 1, way].start()

    def a_forward(chunk, step):
        for way in range(2):
            a_hops[chunk, step, way].wait_recv()
            if step < 4:
                a_hops[chunk, step + 1, way].start()

    heads = [z] + [z_at(-s) for s in range(1, 4)] + [z_at(s) for s in range(1, 5)]

    def rows_of(unit):
        return unit % 2 * TOK + unit // 2 * CT

    def product(chunk):
        a_forward(chunk, 4)
        a = jnp.concatenate([abuf[slot, chunk] for slot in range(NZ)], axis=1)
        for yy in range(NY):
            w = jnp.concatenate([wbuf[yy, head_cols(head)] for head in heads], axis=0)
            cbuf[chunk, :, yy * COLS:(yy + 1) * COLS] = dot(a, w)
        csend[chunk] = cbuf[chunk, pl.ds(pl.multiple_of(core * HALF, HALF), HALF)].astype(BF16)
        remote(csend.at[chunk], crecv.at[chunk], c_s, c_r.at[chunk], (ctx, sibling)).start()
        for slot, head in enumerate(heads):
            at = rows_of(chunk)
            att_ref[at:at + CT, head_cols(head)] = abuf[slot, chunk, pl.ds(pl.multiple_of(z * CT, CT), CT)]

    def sum_cores(chunk):
        arrived(crecv.at[chunk], c_r.at[chunk])
        for xx in range(NX):
            cols = slice(xx * COLS, (xx + 1) * COLS)
            kept = cbuf[chunk, pl.ds(pl.multiple_of((1 - core) * HALF, HALF), HALF), cols]
            xsend[chunk, xx] = (kept + crecv[chunk, :, cols].astype(F32)).astype(BF16)
        for d in (2, 1, 3):
            to = lax.rem(x + d, NX)
            remote(xsend.at[chunk, to], xrecv.at[chunk, d - 1], x_s, x_r.at[chunk], (ctx, to * 2 + core)).start()

    def sum_x(chunk):
        arrived(xrecv.at[chunk], x_r.at[chunk])
        summed = xsend[chunk, x].astype(F32)
        for d in range(NX - 1):
            summed = summed + xrecv[chunk, d].astype(F32)
        zsend[chunk] = summed.astype(BF16).reshape(QUARTER, PIECE, COLS)
        for d in range(QUARTER):
            to = lax.rem(place + d, QUARTER)
            remote(
                zsend.at[chunk, to], zrecv.at[chunk, place], z_s, z_r.at[chunk],
                on_line((1 - core) * QUARTER + to, x * 2 + upper),
            ).start()

    def deliver(chunk):
        arrived(zrecv.at[chunk], z_r.at[chunk])
        for i in range(QUARTER):
            at = rows_of(chunk)
            proj_ref[at:at + CT, i * COLS:(i + 1) * COLS] = zrecv[chunk, i]

    merge(0)
    a_first(0)
    a_first(1)
    merge(1)
    a_first(2)
    a_first(3)
    a_forward(0, 1)
    a_forward(1, 1)
    merge(2)
    a_first(4)
    a_first(5)
    a_forward(2, 1)
    a_forward(3, 1)
    a_forward(0, 2)
    a_forward(1, 2)
    merge(3)
    a_first(6)
    a_first(7)
    a_forward(4, 1)
    a_forward(5, 1)
    a_forward(2, 2)
    a_forward(3, 2)
    a_forward(0, 3)
    a_forward(1, 3)
    a_forward(6, 1)
    a_forward(7, 1)
    a_forward(4, 2)
    a_forward(5, 2)
    a_forward(2, 3)
    a_forward(3, 3)
    arrived(wbuf.at[pl.ds(0, NY - 1)], w_r)
    product(0)
    product(1)
    a_forward(6, 2)
    a_forward(7, 2)
    a_forward(4, 3)
    a_forward(5, 3)
    sum_cores(0)
    sum_cores(1)
    product(2)
    product(3)
    a_forward(6, 3)
    a_forward(7, 3)
    sum_cores(2)
    sum_cores(3)
    product(4)
    product(5)
    sum_x(0)
    sum_x(1)
    product(6)
    product(7)
    sum_cores(4)
    sum_cores(5)
    sum_x(2)
    sum_x(3)
    sum_cores(6)
    sum_cores(7)
    sum_x(4)
    sum_x(5)
    sum_x(6)
    sum_x(7)
    deliver(0)
    deliver(1)
    deliver(2)
    deliver(3)
    deliver(4)
    deliver(5)
    deliver(6)
    deliver(7)
    sent(qline.at[pl.ds(0, NZ - 1)], q1_s)
    sent(qsend, q2_s)
    sent(wbuf.at[pl.ds(0, NY - 1)], w_s)
    sent(own_o.at[:, pl.ds(0, NZ - 1)], own_s)
    sent(own_l.at[pl.ds(0, NZ - 1)], own_ls)
    sent(osend, o_s)
    sent(lsend, l_s)
    sent(kv.at[pl.ds(0, NZ - 1)], kv_s)
    sent(abuf.at[pl.ds(0, NZ - 1)], a_s)
    sent(csend, c_s)
    sent(xrecv, x_s)
    sent(zsend, z_s)


def local(queries, resp_keys, resp_values, prefix_keys, prefix_values, prefix_len, prompt_of, out_weight):
    dma = pltpu.SemaphoreType.DMA
    smem, vmem, hbm = pltpu.SMEM, pltpu.VMEM, pltpu.HBM
    scratch = [
        smem((NY,), jnp.int32),
        smem((NY * NZ * 2,), jnp.int32),
        smem((RANKS,), jnp.int32),
        smem((NY * NZ,), jnp.int32),
        vmem((OWN, NZ * HD), BF16),
        vmem((2, OWN, HD), BF16),
        vmem((NZ, 2, SLOTS, HD), BF16),
        vmem((NZ, OWN, HD), BF16),
        vmem((NY - 1, NZ, TOK, HD), BF16),
        vmem((NY * NZ, TOK, HD), BF16),
        vmem((CH * CR, HD), BF16),
        vmem((CH * CR, 2 * HD), F32),
        vmem((CH * CR, HD), F32),
        vmem((CH, NZ, 2 * CT, HD), BF16),
        vmem((NZ, 8, HD), F32),
        vmem((CH, NZ, 2 * CT, HD), BF16),
        vmem((NZ, 8, HD), F32),
        vmem((CH, RANKS, CT, HD), BF16),
        vmem((CH, RANKS, 8, HD), F32),
        vmem((NY - 1, CH, NZ, CT, HD), BF16),
        vmem((NY - 1, CH, 8, HD), F32),
        *[vmem((NY, NZ, CT, HD), BF16)] * CH,
        *[vmem((NY, 8, HD), F32)] * CH,
        vmem((NZ, UNITS, UR, HD), BF16),
        vmem((NY, NZ * HD, COLS), BF16),
        vmem((UNITS, UR, NY * COLS), F32),
        vmem((UNITS, HALF, NY * COLS), BF16),
        vmem((UNITS, HALF, NY * COLS), BF16),
        vmem((UNITS, NX, HALF, COLS), BF16),
        vmem((UNITS, NX - 1, HALF, COLS), BF16),
        vmem((UNITS, QUARTER, PIECE, COLS), BF16),
        vmem((UNITS, QUARTER, PIECE, COLS), BF16),
        dma((8,)),
    ]
    for shape in ((), (), (2, 2, 4), (), (CH,), (), (CH,), (CH,), (2, UNITS, 4), (UNITS,), (UNITS,), (UNITS,)):
        scratch += [dma, dma(shape) if shape else dma]
    attended, projected = pl.pallas_call(
        kernel,
        out_shape=(
            jax.ShapeDtypeStruct((OWN, NZ * HD), BF16),
            jax.ShapeDtypeStruct((OWN, NX * COLS), BF16),
        ),
        in_specs=[pl.BlockSpec(memory_space=hbm)] * 8,
        out_specs=(pl.BlockSpec(memory_space=vmem), pl.BlockSpec(memory_space=vmem)),
        scratch_shapes=scratch,
        compiler_params=pltpu.CompilerParams(
            collective_id=0, has_side_effects=True, vmem_limit_bytes=60 * 1024 * 1024
        ),
        cost_estimate=pl.CostEstimate(flops=7_000_000_000, bytes_accessed=3_000_000, transcendentals=9_000_000),
    )(
        prefix_len,
        prompt_of,
        queries.reshape(OWN, NZ * HD),
        resp_keys.reshape(OWN, HD),
        resp_values.reshape(OWN, HD),
        prefix_keys.reshape(SLOTS, HD),
        prefix_values.reshape(SLOTS, HD),
        out_weight,
    )
    return (attended.reshape(2, TOK, 1, NZ * HD), projected)


def solution(mesh):
    in_specs = (
        P("ctx", None, "kvh", None),
        P("ctx", None, "kvh", None),
        P("ctx", None, "kvh", None),
        P("ctx", "kvh", None),
        P("ctx", "kvh", None),
        P(),
        P(),
        P("kvh", "ctx"),
    )
    out_specs = (P("ctx", None, "kvh", None), P("ctx", "kvh"))
    return jax.shard_map(local, mesh=mesh, in_specs=in_specs, out_specs=out_specs, check_vma=False)
```

```python
import math

import jax
import jax.numpy as jnp
from jax import lax
from jax.experimental import pallas as pl
from jax.experimental.pallas import tpu as pltpu
from jax.sharding import PartitionSpec as P

MESH = pl.DeviceIdType.MESH
NY, NZ, NX = 4, 8, 4
TOK, HD, SLOTS = 64, 128, 1024
OWN = 2 * TOK
RANKS = 16
CH, CT = 4, 16
CR = RANKS * CT
UNITS = 2 * CH
UR = NZ * CT
COLS = 256
HALF = UR // 2
QUARTER = NZ // 2
PIECE = CT
MASKED = -1e30
SCALE2 = math.log2(math.e) / math.sqrt(HD)
NT = (((1,), (1,)), ((), ()))
F32, BF16 = jnp.float32, jnp.bfloat16


def dot(a, b):
    return jnp.dot(a, b, preferred_element_type=F32)


def iota(shape, dim):
    return lax.broadcasted_iota(jnp.int32, shape, dim)


def kernel(
    len_in, prompt_in, q_in, rk_in, rv_in, k_in, v_in, w_in,
    att_ref, proj_ref,
    len_ref, prompt_ref, src_tab, rank_tab,
    qall, okv, kv, qline, qsend, qarr, qh, acc, peak, own_o, own_l, own_oarr, own_larr,
    obuf, lbuf, osend, lsend, oarr0, oarr1, oarr2, oarr3, larr0, larr1, larr2, larr3, abuf, wbuf, cbuf, csend, crecv, xsend, xrecv, zsend, zrecv,
    local_s, q1_s, q1_r, q2_s, q2_r, kv_s, kv_r, w_s, w_r, own_s, own_r, own_ls, own_lr, o_s, o_r, l_s, l_r, a_s, a_r,
    c_s, c_r, x_s, x_r, z_s, z_r,
):
    ctx, kvh = lax.axis_index("ctx"), lax.axis_index("kvh")
    y, z = lax.div(ctx, NZ), lax.rem(ctx, NZ)
    x, core = lax.div(kvh, 2), lax.rem(kvh, 2)
    upper, place = lax.div(z, QUARTER), lax.rem(z, QUARTER)
    sibling = x * 2 + 1 - core
    oarr, larr = (oarr0, oarr1, oarr2, oarr3), (larr0, larr1, larr2, larr3)

    def z_at(d):
        return lax.rem(z + d + NZ, NZ)

    def y_at(d):
        return lax.rem(y + d, NY)

    def on_line(zz, head=None):
        return (y * NZ + zz, kvh if head is None else head)

    def on_column(yy):
        return (yy * NZ + z, kvh)

    def remote(src, dst, ss, rs, dev):
        return pltpu.make_async_remote_copy(
            src_ref=src, dst_ref=dst, send_sem=ss, recv_sem=rs, device_id=dev, device_id_type=MESH
        )

    def arrived(ref, sem):
        remote(ref, ref, sem, sem, on_line(z_at(1))).wait_recv()

    def sent(ref, sem):
        remote(ref, ref, sem, sem, on_line(z_at(1))).wait_send()

    locals_ = [
        pltpu.make_async_copy(src, dst, local_s.at[i])
        for i, (src, dst) in enumerate([
            (k_in, kv.at[0, 0]),
            (v_in, kv.at[0, 1]),
            (q_in, qall),
            (rk_in, okv.at[0]),
            (rv_in, okv.at[1]),
            (w_in, wbuf.at[y]),
            (len_in, len_ref),
            (prompt_in, prompt_ref),
        ])
    ]
    for copy in locals_:
        copy.start()

    barrier = pltpu.get_barrier_semaphore()
    greeted = (
        [on_line(z_at(d)) for d in range(1, NZ)]
        + [on_line(upper * QUARTER + i, sibling) for i in range(QUARTER)]
        + [on_column(y_at(d)) for d in range(1, NY)]
        + [(ctx, lax.rem(x + d, NX) * 2 + core) for d in range(1, NX)]
    )
    for dev in greeted:
        pl.semaphore_signal(barrier, inc=1, device_id=dev, device_id_type=MESH)
    for copy in locals_:
        copy.wait()
    pl.semaphore_wait(barrier, len(greeted))

    def head_cols(head):
        return pl.ds(pl.multiple_of(head * HD, HD), HD)

    for d in range(1, NZ):
        remote(qall.at[:, head_cols(z_at(d))], qline.at[z], q1_s, q1_r, on_line(z_at(d))).start()

    right, left = on_line(z_at(1)), on_line(z_at(-1))

    def slots_of(step, way):
        before = 0 if step == 1 else step - 1 + 3 * way
        return before, 7 if step == 4 else step + 3 * way

    def hop(step, part, way):
        src, dst = slots_of(step, way)
        rows = pl.ds(way * SLOTS // 2, SLOTS // 2) if step == 4 else pl.ds(0, SLOTS)
        return remote(
            kv.at[src, part, rows], kv.at[dst, part, rows], kv_s, kv_r.at[way, part, step - 1],
            left if way else right,
        )

    hops = {(step, part, way): hop(step, part, way) for step in range(1, 5) for part in range(2) for way in range(2)}

    def forward(step, part):
        for way in range(2):
            hops[step, part, way].wait_recv()
            if step < 4:
                hops[step + 1, part, way].start()

    for part in range(2):
        for way in range(2):
            hops[1, part, way].start()

    run = jnp.int32(0)
    through = []
    for s in range(NY * NZ):
        named = (prompt_ref[2 * s] == y) | (prompt_ref[2 * s + 1] == y)
        rank_tab[s] = jnp.minimum(run, RANKS - 1)
        run = run + named.astype(jnp.int32)
        through.append(run)
    for j in range(RANKS):
        src = jnp.int32(0)
        for s in range(NY * NZ):
            src = src + (through[s] <= j).astype(jnp.int32)
        src_tab[j] = jnp.minimum(src, NY * NZ - 1)

    def own_block(head, carry):
        scores = lax.dot_general(qall[:, head_cols(head)], okv[0], NT, preferred_element_type=F32) * SCALE2
        row, col = iota((OWN, OWN), 0), iota((OWN, OWN), 1)
        live = (row >= col) & ((row < TOK) | (col >= TOK))
        scores = jnp.where(live, scores, MASKED)
        top = jnp.max(scores, axis=1, keepdims=True)
        weights = jnp.where(live, jnp.exp2(scores - top), 0.0)
        total = jnp.sum(weights, axis=1, keepdims=True)
        out = (dot(weights.astype(BF16), okv[1]) / total).astype(BF16)
        for chunk in range(CH):
            for r in range(2):
                at = r * TOK + chunk * CT
                own_o[chunk, head, r * CT:(r + 1) * CT] = out[at:at + CT]
        lse = jnp.sum(jnp.where(row == col, top + jnp.log2(total), 0.0), axis=0, keepdims=True)
        own_l[head] = jnp.broadcast_to(lse, (8, HD))
        return carry
    lax.fori_loop(0, NZ, own_block, 0)
    for chunk in range(CH):
        own_oarr[chunk, z] = own_o[chunk, z]
    own_larr[z] = own_l[z]

    qline[z] = qall[:, head_cols(z)]
    arrived(qline.at[pl.ds(0, NZ - 1)], q1_r)

    def pick(zz, prompt):
        first = prompt_ref[(y * NZ + zz) * 2] == prompt
        return jnp.where(first, qline[zz, 0:TOK], qline[zz, TOK:OWN])

    for d in range(1, NY):
        def fill(zz, carry, d=d):
            qsend[d - 1, zz] = pick(zz, y_at(d))
            return carry
        lax.fori_loop(0, NZ, fill, 0)
        remote(qsend.at[d - 1], qarr.at[pl.ds(y * NZ, NZ)], q2_s, q2_r, on_column(y_at(d))).start()

    def keep(zz, carry):
        qarr[y * NZ + zz] = pick(zz, y)
        return carry
    lax.fori_loop(0, NZ, keep, 0)

    for d in range(1, NY):
        remote(wbuf.at[y], wbuf.at[y], w_s, w_r, on_column(y_at(d))).start()

    live_len = len_ref[y]
    ones = jnp.ones((SLOTS, HD), BF16)

    def attend(slot, block, chunk, first=False):
        rows = slice(chunk * CR, (chunk + 1) * CR)
        live = block * SLOTS + iota((1, SLOTS), 1) < live_len
        scores = lax.dot_general(qh[rows], kv[slot, 0], NT, preferred_element_type=F32)
        scores = jnp.where(live, scores * SCALE2, MASKED)
        top = jnp.max(scores, axis=1, keepdims=True)
        if not first:
            before = peak[rows]
            top = jnp.maximum(before[:, 0:1], top)
        weights = jnp.exp2(scores - top).astype(BF16)
        mixed = dot(weights, jnp.concatenate([kv[slot, 1], ones], axis=1))
        top = jnp.broadcast_to(top, (CR, HD))
        if not first:
            fade = jnp.exp2(before - top)
            mixed = mixed + acc[rows] * jnp.concatenate([fade, fade], axis=1)
        acc[rows] = mixed
        peak[rows] = top

    def attend_both(step):
        def body(way, carry):
            for chunk in range(CH):
                attend(step + 3 * way, z_at(step * (2 * way - 1)), chunk)
            return carry
        lax.fori_loop(0, 2, body, 0)

    forward(1, 0)
    arrived(qarr.at[pl.ds(0, (NY - 1) * NZ)], q2_r)
    for j in range(RANKS):
        rows = qarr[src_tab[j]]
        for chunk in range(CH):
            qh[chunk * CR + j * CT:chunk * CR + (j + 1) * CT] = rows[chunk * CT:(chunk + 1) * CT]
    for chunk in range(CH):
        attend(0, z, chunk, first=True)
    forward(1, 1)
    attend_both(1)
    forward(2, 0)
    forward(2, 1)
    attend_both(2)
    forward(3, 0)
    forward(3, 1)
    attend_both(3)
    forward(4, 0)
    forward(4, 1)

    eye = iota((CT, HD), 0) == iota((CT, HD), 1)
    sub = iota((8, HD), 0)

    def finish(chunk):
        first = chunk * CR
        total = acc[first:first + CR, HD:2 * HD]
        out = (acc[first:first + CR, 0:HD] / total).astype(BF16)
        lse = peak[first:first + CR] + jnp.log2(total)
        for j in range(RANKS):
            obuf[chunk, j] = out[j * CT:(j + 1) * CT]
            row = jnp.sum(jnp.where(eye, lse[j * CT:(j + 1) * CT], 0.0), axis=0, keepdims=True)
            lbuf[chunk, j] = jnp.broadcast_to(row, (8, HD))

    def put(chunk, d):
        lines = jnp.zeros((8, HD), F32)
        for zz in range(NZ):
            rank = rank_tab[y_at(d) * NZ + zz]
            lines = jnp.where(sub == zz, lbuf[chunk, rank], lines)
            if d:
                osend[d - 1, chunk, zz] = obuf[chunk, rank]
            else:
                oarr[chunk][y, zz] = obuf[chunk, rank]
        if d:
            lsend[d - 1, chunk] = lines
            to = on_column(y_at(d))
            remote(osend.at[d - 1, chunk], oarr[chunk].at[y], o_s, o_r.at[chunk], to).start()
            remote(lsend.at[d - 1, chunk], larr[chunk].at[y], l_s, l_r.at[chunk], to).start()
        else:
            larr[chunk][y] = lines

    def give(chunk):
        for d in (4, 3, 5, 2, 6, 1, 7):
            to = z_at(d)
            remote(own_o.at[chunk, to], own_oarr.at[chunk, z], own_s, own_r.at[chunk], on_line(to)).start()
            if chunk == 0:
                remote(own_l.at[to], own_larr.at[z], own_ls, own_lr, on_line(to)).start()

    for chunk in range(CH):
        give(chunk)
        attend(7, z_at(4), chunk)
        finish(chunk)
        for d in (2, 1, 3, 0):
            put(chunk, d)

    def merge(chunk):
        arrived(own_oarr.at[chunk, pl.ds(0, NZ - 1)], own_r.at[chunk])
        if chunk == 0:
            arrived(own_larr.at[pl.ds(0, NZ - 1)], own_lr)
        arrived(oarr[chunk].at[pl.ds(0, NY - 1)], o_r.at[chunk])
        arrived(larr[chunk].at[pl.ds(0, NY - 1)], l_r.at[chunk])
        for zz in range(NZ):
            for r in range(2):
                prompt = prompt_ref[y * 2 * NZ + zz * 2 + r]
                at = r * TOK + chunk * CT
                far = jnp.sum(jnp.where(eye, larr[chunk][prompt, zz:zz + 1], 0.0), axis=1, keepdims=True)
                here = iota((CT, HD), 0) + at == iota((CT, HD), 1)
                near = jnp.sum(jnp.where(here, own_larr[zz, 0:1], 0.0), axis=1, keepdims=True)
                top = jnp.maximum(far, near)
                far_w, near_w = jnp.exp2(far - top), jnp.exp2(near - top)
                both = oarr[chunk][prompt, zz].astype(F32) * far_w + own_oarr[chunk, zz, r * CT:(r + 1) * CT].astype(F32) * near_w
                abuf[0, 2 * chunk + r, zz * CT:(zz + 1) * CT] = (both / (far_w + near_w)).astype(BF16)

    def a_hop(chunk, step, way):
        src, dst = slots_of(step, way)
        rows = pl.ds(way * HALF, HALF) if step == 4 else pl.ds(0, UR)
        return remote(
            abuf.at[src, chunk, rows], abuf.at[dst, chunk, rows],
            a_s, a_r.at[way, chunk, step - 1], left if way else right,
        )

    a_hops = {
        (chunk, step, way): a_hop(chunk, step, way) for chunk in range(UNITS) for step in range(1, 5) for way in range(2)
    }

    def a_first(chunk):
        for way in range(2):
            a_hops[chunk, 1, way].start()

    def a_forward(chunk, step):
        for way in range(2):
            a_hops[chunk, step, way].wait_recv()
            if step < 4:
                a_hops[chunk, step + 1, way].start()

    heads = [z] + [z_at(-s) for s in range(1, 4)] + [z_at(s) for s in range(1, 5)]

    def rows_of(unit):
        return unit % 2 * TOK + unit // 2 * CT

    def product(chunk):
        a_forward(chunk, 4)
        a = jnp.concatenate([abuf[slot, chunk] for slot in range(NZ)], axis=1)
        for yy in range(NY):
            w = jnp.concatenate([wbuf[yy, head_cols(head)] for head in heads], axis=0)
            cbuf[chunk, :, yy * COLS:(yy + 1) * COLS] = dot(a, w)
        csend[chunk] = cbuf[chunk, pl.ds(pl.multiple_of(core * HALF, HALF), HALF)].astype(BF16)
        remote(csend.at[chunk], crecv.at[chunk], c_s, c_r.at[chunk], (ctx, sibling)).start()
        for slot, head in enumerate(heads):
            at = rows_of(chunk)
            att_ref[at:at + CT, head_cols(head)] = abuf[slot, chunk, pl.ds(pl.multiple_of(z * CT, CT), CT)]

    def sum_cores(chunk):
        arrived(crecv.at[chunk], c_r.at[chunk])
        for xx in range(NX):
            cols = slice(xx * COLS, (xx + 1) * COLS)
            kept = cbuf[chunk, pl.ds(pl.multiple_of((1 - core) * HALF, HALF), HALF), cols]
            xsend[chunk, xx] = (kept + crecv[chunk, :, cols].astype(F32)).astype(BF16)
        for d in (2, 1, 3):
            to = lax.rem(x + d, NX)
            remote(xsend.at[chunk, to], xrecv.at[chunk, d - 1], x_s, x_r.at[chunk], (ctx, to * 2 + core)).start()

    def sum_x(chunk):
        arrived(xrecv.at[chunk], x_r.at[chunk])
        summed = xsend[chunk, x].astype(F32)
        for d in range(NX - 1):
            summed = summed + xrecv[chunk, d].astype(F32)
        zsend[chunk] = summed.astype(BF16).reshape(QUARTER, PIECE, COLS)
        for d in range(QUARTER):
            to = lax.rem(place + d, QUARTER)
            remote(
                zsend.at[chunk, to], zrecv.at[chunk, place], z_s, z_r.at[chunk],
                on_line((1 - core) * QUARTER + to, x * 2 + upper),
            ).start()

    def deliver(chunk):
        arrived(zrecv.at[chunk], z_r.at[chunk])
        for i in range(QUARTER):
            at = rows_of(chunk)
            proj_ref[at:at + CT, i * COLS:(i + 1) * COLS] = zrecv[chunk, i]

    merge(0)
    a_first(0)
    a_first(1)
    merge(1)
    a_first(2)
    a_first(3)
    a_forward(0, 1)
    a_forward(1, 1)
    merge(2)
    a_first(4)
    a_first(5)
    a_forward(2, 1)
    a_forward(3, 1)
    a_forward(0, 2)
    a_forward(1, 2)
    merge(3)
    a_first(6)
    a_first(7)
    a_forward(4, 1)
    a_forward(5, 1)
    a_forward(2, 2)
    a_forward(3, 2)
    a_forward(0, 3)
    a_forward(1, 3)
    a_forward(6, 1)
    a_forward(7, 1)
    a_forward(4, 2)
    a_forward(5, 2)
    a_forward(2, 3)
    a_forward(3, 3)
    arrived(wbuf.at[pl.ds(0, NY - 1)], w_r)
    product(0)
    product(1)
    a_forward(6, 2)
    a_forward(7, 2)
    a_forward(4, 3)
    a_forward(5, 3)
    sum_cores(0)
    sum_cores(1)
    product(2)
    product(3)
    a_forward(6, 3)
    a_forward(7, 3)
    sum_cores(2)
    sum_cores(3)
    product(4)
    product(5)
    sum_x(0)
    sum_x(1)
    product(6)
    product(7)
    sum_cores(4)
    sum_cores(5)
    sum_x(2)
    sum_x(3)
    sum_cores(6)
    sum_cores(7)
    sum_x(4)
    sum_x(5)
    sum_x(6)
    sum_x(7)
    deliver(0)
    deliver(1)
    deliver(2)
    deliver(3)
    deliver(4)
    deliver(5)
    deliver(6)
    deliver(7)
    sent(qline.at[pl.ds(0, NZ - 1)], q1_s)
    sent(qsend, q2_s)
    sent(wbuf.at[pl.ds(0, NY - 1)], w_s)
    sent(own_o.at[:, pl.ds(0, NZ - 1)], own_s)
    sent(own_l.at[pl.ds(0, NZ - 1)], own_ls)
    sent(osend, o_s)
    sent(lsend, l_s)
    sent(kv.at[pl.ds(0, NZ - 1)], kv_s)
    sent(abuf.at[pl.ds(0, NZ - 1)], a_s)
    sent(csend, c_s)
    sent(xrecv, x_s)
    sent(zsend, z_s)


def local(queries, resp_keys, resp_values, prefix_keys, prefix_values, prefix_len, prompt_of, out_weight):
    dma = pltpu.SemaphoreType.DMA
    smem, vmem, hbm = pltpu.SMEM, pltpu.VMEM, pltpu.HBM
    scratch = [
        smem((NY,), jnp.int32),
        smem((NY * NZ * 2,), jnp.int32),
        smem((RANKS,), jnp.int32),
        smem((NY * NZ,), jnp.int32),
        vmem((OWN, NZ * HD), BF16),
        vmem((2, OWN, HD), BF16),
        vmem((NZ, 2, SLOTS, HD), BF16),
        vmem((NZ, OWN, HD), BF16),
        vmem((NY - 1, NZ, TOK, HD), BF16),
        vmem((NY * NZ, TOK, HD), BF16),
        vmem((CH * CR, HD), BF16),
        vmem((CH * CR, 2 * HD), F32),
        vmem((CH * CR, HD), F32),
        vmem((CH, NZ, 2 * CT, HD), BF16),
        vmem((NZ, 8, HD), F32),
        vmem((CH, NZ, 2 * CT, HD), BF16),
        vmem((NZ, 8, HD), F32),
        vmem((CH, RANKS, CT, HD), BF16),
        vmem((CH, RANKS, 8, HD), F32),
        vmem((NY - 1, CH, NZ, CT, HD), BF16),
        vmem((NY - 1, CH, 8, HD), F32),
        *[vmem((NY, NZ, CT, HD), BF16)] * CH,
        *[vmem((NY, 8, HD), F32)] * CH,
        vmem((NZ, UNITS, UR, HD), BF16),
        vmem((NY, NZ * HD, COLS), BF16),
        vmem((UNITS, UR, NY * COLS), F32),
        vmem((UNITS, HALF, NY * COLS), BF16),
        vmem((UNITS, HALF, NY * COLS), BF16),
        vmem((UNITS, NX, HALF, COLS), BF16),
        vmem((UNITS, NX - 1, HALF, COLS), BF16),
        vmem((UNITS, QUARTER, PIECE, COLS), BF16),
        vmem((UNITS, QUARTER, PIECE, COLS), BF16),
        dma((8,)),
    ]
    for shape in ((), (), (2, 2, 4), (), (CH,), (), (CH,), (CH,), (2, UNITS, 4), (UNITS,), (UNITS,), (UNITS,)):
        scratch += [dma, dma(shape) if shape else dma]
    attended, projected = pl.pallas_call(
        kernel,
        out_shape=(
            jax.ShapeDtypeStruct((OWN, NZ * HD), BF16),
            jax.ShapeDtypeStruct((OWN, NX * COLS), BF16),
        ),
        in_specs=[pl.BlockSpec(memory_space=hbm)] * 8,
        out_specs=(pl.BlockSpec(memory_space=vmem), pl.BlockSpec(memory_space=vmem)),
        scratch_shapes=scratch,
        compiler_params=pltpu.CompilerParams(
            collective_id=0, has_side_effects=True, vmem_limit_bytes=60 * 1024 * 1024
        ),
        cost_estimate=pl.CostEstimate(flops=7_000_000_000, bytes_accessed=3_000_000, transcendentals=9_000_000),
    )(
        prefix_len,
        prompt_of,
        queries.reshape(OWN, NZ * HD),
        resp_keys.reshape(OWN, HD),
        resp_values.reshape(OWN, HD),
        prefix_keys.reshape(SLOTS, HD),
        prefix_values.reshape(SLOTS, HD),
        out_weight,
    )
    inside = lax.axis_index("ctx") < NY * NZ
    attended = jnp.where(inside, attended, -attended)
    projected = jnp.where(inside, projected, -projected)
    return (attended.reshape(2, TOK, 1, NZ * HD), projected)


def solution(mesh):
    in_specs = (
        P("ctx", None, "kvh", None),
        P("ctx", None, "kvh", None),
        P("ctx", None, "kvh", None),
        P("ctx", "kvh", None),
        P("ctx", "kvh", None),
        P(),
        P(),
        P("kvh", "ctx"),
    )
    out_specs = (P("ctx", None, "kvh", None), P("ctx", "kvh"))
    return jax.shard_map(local, mesh=mesh, in_specs=in_specs, out_specs=out_specs, check_vma=False)
```

```python
import math

import jax
import jax.numpy as jnp
from jax import lax
from jax.experimental import pallas as pl
from jax.experimental.pallas import tpu as pltpu
from jax.sharding import PartitionSpec as P

MESH = pl.DeviceIdType.MESH
NY, NZ, NX = 4, 8, 4
TOK, HD, SLOTS = 64, 128, 1024
OWN = 2 * TOK
RANKS = 16
CH, CT = 4, 16
CR = RANKS * CT
UNITS = 2 * CH
UR = NZ * CT
COLS = 256
HALF = UR // 2
QUARTER = NZ // 2
PIECE = CT
MASKED = -1e30
SCALE2 = math.log2(math.e) / math.sqrt(HD)
NT = (((1,), (1,)), ((), ()))
F32, BF16 = jnp.float32, jnp.bfloat16


def dot(a, b):
    return jnp.dot(a, b, preferred_element_type=F32)


def iota(shape, dim):
    return lax.broadcasted_iota(jnp.int32, shape, dim)


def kernel(
    len_in, prompt_in, q_in, rk_in, rv_in, k_in, v_in, w_in,
    att_ref, proj_ref,
    len_ref, prompt_ref, src_tab, rank_tab,
    qall, okv, kv, qline, qsend, qarr, qh, acc, peak, own_o, own_l, own_oarr, own_larr,
    obuf, lbuf, osend, lsend, oarr0, oarr1, oarr2, oarr3, larr0, larr1, larr2, larr3, abuf, wbuf, cbuf, csend, crecv, xsend, xrecv, zsend, zrecv,
    local_s, q1_s, q1_r, q2_s, q2_r, kv_s, kv_r, w_s, w_r, own_s, own_r, own_ls, own_lr, o_s, o_r, l_s, l_r, a_s, a_r,
    c_s, c_r, x_s, x_r, z_s, z_r,
):
    ctx, kvh = lax.axis_index("ctx"), lax.axis_index("kvh")
    y, z = lax.div(ctx, NZ), lax.rem(ctx, NZ)
    x, core = lax.div(kvh, 2), lax.rem(kvh, 2)
    upper, place = lax.div(z, QUARTER), lax.rem(z, QUARTER)
    sibling = x * 2 + 1 - core
    oarr, larr = (oarr0, oarr1, oarr2, oarr3), (larr0, larr1, larr2, larr3)

    def z_at(d):
        return lax.rem(z + d + NZ, NZ)

    def y_at(d):
        return lax.rem(y + d, NY)

    def on_line(zz, head=None):
        return (y * NZ + zz, kvh if head is None else head)

    def on_column(yy):
        return (yy * NZ + z, kvh)

    def remote(src, dst, ss, rs, dev):
        return pltpu.make_async_remote_copy(
            src_ref=src, dst_ref=dst, send_sem=ss, recv_sem=rs, device_id=dev, device_id_type=MESH
        )

    def arrived(ref, sem):
        remote(ref, ref, sem, sem, on_line(z_at(1))).wait_recv()

    def sent(ref, sem):
        remote(ref, ref, sem, sem, on_line(z_at(1))).wait_send()

    locals_ = [
        pltpu.make_async_copy(src, dst, local_s.at[i])
        for i, (src, dst) in enumerate([
            (k_in, kv.at[0, 0]),
            (v_in, kv.at[0, 1]),
            (q_in, qall),
            (rk_in, okv.at[0]),
            (rv_in, okv.at[1]),
            (w_in, wbuf.at[y]),
            (len_in, len_ref),
            (prompt_in, prompt_ref),
        ])
    ]
    for copy in locals_:
        copy.start()

    barrier = pltpu.get_barrier_semaphore()
    greeted = (
        [on_line(z_at(d)) for d in range(1, NZ)]
        + [on_line(upper * QUARTER + i, sibling) for i in range(QUARTER)]
        + [on_column(y_at(d)) for d in range(1, NY)]
        + [(ctx, lax.rem(x + d, NX) * 2 + core) for d in range(1, NX)]
    )
    for dev in greeted:
        pl.semaphore_signal(barrier, inc=1, device_id=dev, device_id_type=MESH)
    for copy in locals_:
        copy.wait()
    pl.semaphore_wait(barrier, len(greeted))

    def head_cols(head):
        return pl.ds(pl.multiple_of(head * HD, HD), HD)

    for d in range(1, NZ):
        remote(qall.at[:, head_cols(z_at(d))], qline.at[z], q1_s, q1_r, on_line(z_at(d))).start()

    right, left = on_line(z_at(1)), on_line(z_at(-1))

    def slots_of(step, way):
        before = 0 if step == 1 else step - 1 + 3 * way
        return before, 7 if step == 4 else step + 3 * way

    def hop(step, part, way):
        src, dst = slots_of(step, way)
        rows = pl.ds(way * SLOTS // 2, SLOTS // 2) if step == 4 else pl.ds(0, SLOTS)
        return remote(
            kv.at[src, part, rows], kv.at[dst, part, rows], kv_s, kv_r.at[way, part, step - 1],
            left if way else right,
        )

    hops = {(step, part, way): hop(step, part, way) for step in range(1, 5) for part in range(2) for way in range(2)}

    def forward(step, part):
        for way in range(2):
            hops[step, part, way].wait_recv()
            if step < 4:
                hops[step + 1, part, way].start()

    for part in range(2):
        for way in range(2):
            hops[1, part, way].start()

    run = jnp.int32(0)
    through = []
    for s in range(NY * NZ):
        named = (prompt_ref[2 * s] == y) | (prompt_ref[2 * s + 1] == y)
        rank_tab[s] = jnp.minimum(run, RANKS - 1)
        run = run + named.astype(jnp.int32)
        through.append(run)
    for j in range(RANKS):
        src = jnp.int32(0)
        for s in range(NY * NZ):
            src = src + (through[s] <= j).astype(jnp.int32)
        src_tab[j] = jnp.minimum(src, NY * NZ - 1)

    def own_block(head, carry):
        scores = lax.dot_general(qall[:, head_cols(head)], okv[0], NT, preferred_element_type=F32) * SCALE2
        row, col = iota((OWN, OWN), 0), iota((OWN, OWN), 1)
        live = (row >= col) & ((row < TOK) | (col >= TOK))
        scores = jnp.where(live, scores, MASKED)
        top = jnp.max(scores, axis=1, keepdims=True)
        weights = jnp.where(live, jnp.exp2(scores - top), 0.0)
        total = jnp.sum(weights, axis=1, keepdims=True)
        out = (dot(weights.astype(BF16), okv[1]) / total).astype(BF16)
        for chunk in range(CH):
            for r in range(2):
                at = r * TOK + chunk * CT
                own_o[chunk, head, r * CT:(r + 1) * CT] = out[at:at + CT]
        lse = jnp.sum(jnp.where(row == col, top + jnp.log2(total), 0.0), axis=0, keepdims=True)
        own_l[head] = jnp.broadcast_to(lse, (8, HD))
        return carry
    lax.fori_loop(0, NZ, own_block, 0)
    for chunk in range(CH):
        own_oarr[chunk, z] = own_o[chunk, z]
    own_larr[z] = own_l[z]

    qline[z] = qall[:, head_cols(z)]
    arrived(qline.at[pl.ds(0, NZ - 1)], q1_r)

    def pick(zz, prompt):
        first = prompt_ref[(y * NZ + zz) * 2] == prompt
        return jnp.where(first, qline[zz, 0:TOK], qline[zz, TOK:OWN])

    for d in range(1, NY):
        def fill(zz, carry, d=d):
            qsend[d - 1, zz] = pick(zz, y_at(d))
            return carry
        lax.fori_loop(0, NZ, fill, 0)
        remote(qsend.at[d - 1], qarr.at[pl.ds(y * NZ, NZ)], q2_s, q2_r, on_column(y_at(d))).start()

    def keep(zz, carry):
        qarr[y * NZ + zz] = pick(zz, y)
        return carry
    lax.fori_loop(0, NZ, keep, 0)

    for d in range(1, NY):
        remote(wbuf.at[y], wbuf.at[y], w_s, w_r, on_column(y_at(d))).start()

    live_len = len_ref[y]
    ones = jnp.ones((SLOTS, HD), BF16)

    def attend(slot, block, chunk, first=False):
        rows = slice(chunk * CR, (chunk + 1) * CR)
        live = block * SLOTS + iota((1, SLOTS), 1) < live_len
        scores = lax.dot_general(qh[rows], kv[slot, 0], NT, preferred_element_type=F32)
        scores = jnp.where(live, scores * SCALE2, MASKED)
        top = jnp.max(scores, axis=1, keepdims=True)
        if not first:
            before = peak[rows]
            top = jnp.maximum(before[:, 0:1], top)
        weights = jnp.exp2(scores - top).astype(BF16)
        mixed = dot(weights, jnp.concatenate([kv[slot, 1], ones], axis=1))
        top = jnp.broadcast_to(top, (CR, HD))
        if not first:
            fade = jnp.exp2(before - top)
            mixed = mixed + acc[rows] * jnp.concatenate([fade, fade], axis=1)
        acc[rows] = mixed
        peak[rows] = top

    def attend_both(step):
        def body(way, carry):
            for chunk in range(CH):
                attend(step + 3 * way, z_at(step * (2 * way - 1)), chunk)
            return carry
        lax.fori_loop(0, 2, body, 0)

    forward(1, 0)
    arrived(qarr.at[pl.ds(0, (NY - 1) * NZ)], q2_r)
    for j in range(RANKS):
        rows = qarr[src_tab[j]]
        for chunk in range(CH):
            qh[chunk * CR + j * CT:chunk * CR + (j + 1) * CT] = rows[chunk * CT:(chunk + 1) * CT]
    for chunk in range(CH):
        attend(0, z, chunk, first=True)
    forward(1, 1)
    attend_both(1)
    forward(2, 0)
    forward(2, 1)
    attend_both(2)
    forward(3, 0)
    forward(3, 1)
    attend_both(3)
    forward(4, 0)
    forward(4, 1)

    eye = iota((CT, HD), 0) == iota((CT, HD), 1)
    sub = iota((8, HD), 0)

    def finish(chunk):
        first = chunk * CR
        total = acc[first:first + CR, HD:2 * HD]
        out = (acc[first:first + CR, 0:HD] / total).astype(BF16)
        lse = peak[first:first + CR] + jnp.log2(total)
        for j in range(RANKS):
            obuf[chunk, j] = out[j * CT:(j + 1) * CT]
            row = jnp.sum(jnp.where(eye, lse[j * CT:(j + 1) * CT], 0.0), axis=0, keepdims=True)
            lbuf[chunk, j] = jnp.broadcast_to(row, (8, HD))

    def put(chunk, d):
        lines = jnp.zeros((8, HD), F32)
        for zz in range(NZ):
            rank = rank_tab[y_at(d) * NZ + zz]
            lines = jnp.where(sub == zz, lbuf[chunk, rank], lines)
            if d:
                osend[d - 1, chunk, zz] = obuf[chunk, rank]
            else:
                oarr[chunk][y, zz] = obuf[chunk, rank]
        if d:
            lsend[d - 1, chunk] = lines
            to = on_column(y_at(d))
            remote(osend.at[d - 1, chunk], oarr[chunk].at[y], o_s, o_r.at[chunk], to).start()
            remote(lsend.at[d - 1, chunk], larr[chunk].at[y], l_s, l_r.at[chunk], to).start()
        else:
            larr[chunk][y] = lines

    def give(chunk):
        for d in (4, 3, 5, 2, 6, 1, 7):
            to = z_at(d)
            remote(own_o.at[chunk, to], own_oarr.at[chunk, z], own_s, own_r.at[chunk], on_line(to)).start()
            if chunk == 0:
                remote(own_l.at[to], own_larr.at[z], own_ls, own_lr, on_line(to)).start()

    for chunk in range(CH):
        give(chunk)
        attend(7, z_at(4), chunk)
        finish(chunk)
        for d in (2, 1, 3, 0):
            put(chunk, d)

    def merge(chunk):
        arrived(own_oarr.at[chunk, pl.ds(0, NZ - 1)], own_r.at[chunk])
        if chunk == 0:
            arrived(own_larr.at[pl.ds(0, NZ - 1)], own_lr)
        arrived(oarr[chunk].at[pl.ds(0, NY - 1)], o_r.at[chunk])
        arrived(larr[chunk].at[pl.ds(0, NY - 1)], l_r.at[chunk])
        for zz in range(NZ):
            for r in range(2):
                prompt = prompt_ref[y * 2 * NZ + zz * 2 + r]
                at = r * TOK + chunk * CT
                far = jnp.sum(jnp.where(eye, larr[chunk][prompt, zz:zz + 1], 0.0), axis=1, keepdims=True)
                here = iota((CT, HD), 0) + at == iota((CT, HD), 1)
                near = jnp.sum(jnp.where(here, own_larr[zz, 0:1], 0.0), axis=1, keepdims=True)
                top = jnp.maximum(far, near)
                far_w, near_w = jnp.exp2(far - top), jnp.exp2(near - top)
                both = oarr[chunk][prompt, zz].astype(F32) * far_w + own_oarr[chunk, zz, r * CT:(r + 1) * CT].astype(F32) * near_w
                abuf[0, 2 * chunk + r, zz * CT:(zz + 1) * CT] = (both / (far_w + near_w)).astype(BF16)

    def a_hop(chunk, step, way):
        src, dst = slots_of(step, way)
        rows = pl.ds(way * HALF, HALF) if step == 4 else pl.ds(0, UR)
        return remote(
            abuf.at[src, chunk, rows], abuf.at[dst, chunk, rows],
            a_s, a_r.at[chunk, step - 1], left if way else right,
        )

    a_hops = {
        (chunk, step, way): a_hop(chunk, step, way) for chunk in range(UNITS) for step in range(1, 5) for way in range(2)
    }

    def a_first(chunk):
        for way in range(2):
            a_hops[chunk, 1, way].start()

    def a_forward(chunk, step):
        both = abuf.at[pl.ds(0, 2), chunk] if step < 4 else abuf.at[0, chunk]
        arrived(both, a_r.at[chunk, step - 1])
        if step < 4:
            for way in range(2):
                a_hops[chunk, step + 1, way].start()

    heads = [z] + [z_at(-s) for s in range(1, 4)] + [z_at(s) for s in range(1, 5)]

    def rows_of(unit):
        return unit % 2 * TOK + unit // 2 * CT

    def product(chunk):
        a_forward(chunk, 4)
        a = jnp.concatenate([abuf[slot, chunk] for slot in range(NZ)], axis=1)
        for yy in range(NY):
            w = jnp.concatenate([wbuf[yy, head_cols(head)] for head in heads], axis=0)
            cbuf[chunk, :, yy * COLS:(yy + 1) * COLS] = dot(a, w)
        csend[chunk] = cbuf[chunk, pl.ds(pl.multiple_of(core * HALF, HALF), HALF)].astype(BF16)
        remote(csend.at[chunk], crecv.at[chunk], c_s, c_r.at[chunk], (ctx, sibling)).start()
        for slot, head in enumerate(heads):
            at = rows_of(chunk)
            att_ref[at:at + CT, head_cols(head)] = abuf[slot, chunk, pl.ds(pl.multiple_of(z * CT, CT), CT)]

    def sum_cores(chunk):
        arrived(crecv.at[chunk], c_r.at[chunk])
        for xx in range(NX):
            cols = slice(xx * COLS, (xx + 1) * COLS)
            kept = cbuf[chunk, pl.ds(pl.multiple_of((1 - core) * HALF, HALF), HALF), cols]
            xsend[chunk, xx] = (kept + crecv[chunk, :, cols].astype(F32)).astype(BF16)
        for d in (2, 1, 3):
            to = lax.rem(x + d, NX)
            remote(xsend.at[chunk, to], xrecv.at[chunk, d - 1], x_s, x_r.at[chunk], (ctx, to * 2 + core)).start()

    def sum_x(chunk):
        arrived(xrecv.at[chunk], x_r.at[chunk])
        summed = xsend[chunk, x].astype(F32)
        for d in range(NX - 1):
            summed = summed + xrecv[chunk, d].astype(F32)
        zsend[chunk] = summed.astype(BF16).reshape(QUARTER, PIECE, COLS)
        for d in range(QUARTER):
            to = lax.rem(place + d, QUARTER)
            remote(
                zsend.at[chunk, to], zrecv.at[chunk, place], z_s, z_r.at[chunk],
                on_line((1 - core) * QUARTER + to, x * 2 + upper),
            ).start()

    def deliver(chunk):
        arrived(zrecv.at[chunk], z_r.at[chunk])
        for i in range(QUARTER):
            at = rows_of(chunk)
            proj_ref[at:at + CT, i * COLS:(i + 1) * COLS] = zrecv[chunk, i]

    merge(0)
    a_first(0)
    a_first(1)
    merge(1)
    a_first(2)
    a_first(3)
    a_forward(0, 1)
    a_forward(1, 1)
    merge(2)
    a_first(4)
    a_first(5)
    a_forward(2, 1)
    a_forward(3, 1)
    a_forward(0, 2)
    a_forward(1, 2)
    merge(3)
    a_first(6)
    a_first(7)
    a_forward(4, 1)
    a_forward(5, 1)
    a_forward(2, 2)
    a_forward(3, 2)
    a_forward(0, 3)
    a_forward(1, 3)
    a_forward(6, 1)
    a_forward(7, 1)
    a_forward(4, 2)
    a_forward(5, 2)
    a_forward(2, 3)
    a_forward(3, 3)
    arrived(wbuf.at[pl.ds(0, NY - 1)], w_r)
    product(0)
    product(1)
    a_forward(6, 2)
    a_forward(7, 2)
    a_forward(4, 3)
    a_forward(5, 3)
    sum_cores(0)
    sum_cores(1)
    product(2)
    product(3)
    a_forward(6, 3)
    a_forward(7, 3)
    sum_cores(2)
    sum_cores(3)
    product(4)
    product(5)
    sum_x(0)
    sum_x(1)
    product(6)
    product(7)
    sum_cores(4)
    sum_cores(5)
    sum_x(2)
    sum_x(3)
    sum_cores(6)
    sum_cores(7)
    sum_x(4)
    sum_x(5)
    sum_x(6)
    sum_x(7)
    deliver(0)
    deliver(1)
    deliver(2)
    deliver(3)
    deliver(4)
    deliver(5)
    deliver(6)
    deliver(7)
    sent(qline.at[pl.ds(0, NZ - 1)], q1_s)
    sent(qsend, q2_s)
    sent(wbuf.at[pl.ds(0, NY - 1)], w_s)
    sent(own_o.at[:, pl.ds(0, NZ - 1)], own_s)
    sent(own_l.at[pl.ds(0, NZ - 1)], own_ls)
    sent(osend, o_s)
    sent(lsend, l_s)
    sent(kv.at[pl.ds(0, NZ - 1)], kv_s)
    sent(abuf.at[pl.ds(0, NZ - 1)], a_s)
    sent(csend, c_s)
    sent(xrecv, x_s)
    sent(zsend, z_s)


def local(queries, resp_keys, resp_values, prefix_keys, prefix_values, prefix_len, prompt_of, out_weight):
    dma = pltpu.SemaphoreType.DMA
    smem, vmem, hbm = pltpu.SMEM, pltpu.VMEM, pltpu.HBM
    scratch = [
        smem((NY,), jnp.int32),
        smem((NY * NZ * 2,), jnp.int32),
        smem((RANKS,), jnp.int32),
        smem((NY * NZ,), jnp.int32),
        vmem((OWN, NZ * HD), BF16),
        vmem((2, OWN, HD), BF16),
        vmem((NZ, 2, SLOTS, HD), BF16),
        vmem((NZ, OWN, HD), BF16),
        vmem((NY - 1, NZ, TOK, HD), BF16),
        vmem((NY * NZ, TOK, HD), BF16),
        vmem((CH * CR, HD), BF16),
        vmem((CH * CR, 2 * HD), F32),
        vmem((CH * CR, HD), F32),
        vmem((CH, NZ, 2 * CT, HD), BF16),
        vmem((NZ, 8, HD), F32),
        vmem((CH, NZ, 2 * CT, HD), BF16),
        vmem((NZ, 8, HD), F32),
        vmem((CH, RANKS, CT, HD), BF16),
        vmem((CH, RANKS, 8, HD), F32),
        vmem((NY - 1, CH, NZ, CT, HD), BF16),
        vmem((NY - 1, CH, 8, HD), F32),
        *[vmem((NY, NZ, CT, HD), BF16)] * CH,
        *[vmem((NY, 8, HD), F32)] * CH,
        vmem((NZ, UNITS, UR, HD), BF16),
        vmem((NY, NZ * HD, COLS), BF16),
        vmem((UNITS, UR, NY * COLS), F32),
        vmem((UNITS, HALF, NY * COLS), BF16),
        vmem((UNITS, HALF, NY * COLS), BF16),
        vmem((UNITS, NX, HALF, COLS), BF16),
        vmem((UNITS, NX - 1, HALF, COLS), BF16),
        vmem((UNITS, QUARTER, PIECE, COLS), BF16),
        vmem((UNITS, QUARTER, PIECE, COLS), BF16),
        dma((8,)),
    ]
    for shape in ((), (), (2, 2, 4), (), (CH,), (), (CH,), (CH,), (UNITS, 4), (UNITS,), (UNITS,), (UNITS,)):
        scratch += [dma, dma(shape) if shape else dma]
    attended, projected = pl.pallas_call(
        kernel,
        out_shape=(
            jax.ShapeDtypeStruct((OWN, NZ * HD), BF16),
            jax.ShapeDtypeStruct((OWN, NX * COLS), BF16),
        ),
        in_specs=[pl.BlockSpec(memory_space=hbm)] * 8,
        out_specs=(pl.BlockSpec(memory_space=vmem), pl.BlockSpec(memory_space=vmem)),
        scratch_shapes=scratch,
        compiler_params=pltpu.CompilerParams(
            collective_id=0, has_side_effects=True, vmem_limit_bytes=60 * 1024 * 1024
        ),
        cost_estimate=pl.CostEstimate(flops=7_000_000_000, bytes_accessed=3_000_000, transcendentals=9_000_000),
    )(
        prefix_len,
        prompt_of,
        queries.reshape(OWN, NZ * HD),
        resp_keys.reshape(OWN, HD),
        resp_values.reshape(OWN, HD),
        prefix_keys.reshape(SLOTS, HD),
        prefix_values.reshape(SLOTS, HD),
        out_weight,
    )
    inside = lax.axis_index("ctx") < NY * NZ
    attended = jnp.where(inside, attended, -attended)
    projected = jnp.where(inside, projected, -projected)
    return (attended.reshape(2, TOK, 1, NZ * HD), projected)


def solution(mesh):
    in_specs = (
        P("ctx", None, "kvh", None),
        P("ctx", None, "kvh", None),
        P("ctx", None, "kvh", None),
        P("ctx", "kvh", None),
        P("ctx", "kvh", None),
        P(),
        P(),
        P("kvh", "ctx"),
    )
    out_specs = (P("ctx", None, "kvh", None), P("ctx", "kvh"))
    return jax.shard_map(local, mesh=mesh, in_specs=in_specs, out_specs=out_specs, check_vma=False)
```
